32 devices in a mesh: grp: 2 (over y), freq: 4 (over z), shot: 2 (over x), rcv: 2 (over core).
Axes of the slice: x: 2, y: 2, z: 4, core: 2. Of those that a mesh axis runs over, the one named last changes fastest.
Arguments:
- data: bfloat16 [2, 256, 32, 4096], P(None, 'freq', ('grp', 'shot'), 'rcv'), parts along dimension 2, may hold values from -6 to 6
- estimate: bfloat16 [2, 256, 32, 4096], P(None, 'freq', ('grp', 'shot'), 'rcv'), parts along dimension 2, may hold values from -0.09375 to 0.09375
- window_data: bfloat16 [2, 256, 32, 16], P(None, 'freq', ('grp', 'shot')), parts along dimension 2, may hold values from -6 to 6
- wavelet: float32 [2, 512], P(None, ('grp', 'freq')), parts along dimension 1, may hold values from -24 to 24
- positions: int32 [32], P(('grp', 'shot')), parts along dimension 0, may hold values from 0 to 4095
- bins: int32 [512], P('grp'), parts along dimension 0, may hold values from 0 to 399
- threshold: int32 [2], P('grp'), parts along dimension 0, may hold values from 8 to 40
- step: float32 [2], P('grp'), parts along dimension 0, may hold values from 0.25 to 1
Outputs:
- primaries: bfloat16 [1024, 32, 4096], P('freq', ('grp', 'shot'), 'rcv'), parts along dimension 1
The draws below stay inside these ranges and needn't reach their ends.
There are 2 independent parts, one for each index of `grp`. The reference program is written for one: setup_inputs(seed, part) draws one part's arguments, and reference() takes and returns one part's arrays. A program takes and returns all parts, laid end to end along the dimension named above; each array names one. Nothing has to cross between parts.
All inputs are finite; a program needn't handle non-finite values.
Results may differ from the reference program's by a relative error of at most 0.0059.
The reference program's roundings to bfloat16 on the way count: a program that leaves them out, or rounds other values in their place, can miss the bound.
Values may be sent and summed in bfloat16 or wider, within the bound.
No kernel may reach another device: no remote copies, remote signals or barrier semaphores. Data moves between devices by JAX's collectives and lax.ppermute only.
A program may use at most 64 MiB of HBM per device.

```python
import math
import jax
import jax.numpy as jnp
from jax import lax

NF = 256
RCV = 4096
NT = 1024
NBIN = 400
ROWS = 16
SHOTS = 16


def touch_ends(result, stream_key, smallest, top_value):
    extent = result.shape
    index_at = [jax.random.randint(jax.random.fold_in(stream_key, axis), (), 0, extent[axis]) for axis in range(len(extent))]
    result = result.at[tuple(index_at)].set(smallest)
    longest = extent.index(max(extent))
    index_at[longest] = (index_at[longest] + 1) % extent[longest]
    return result.at[tuple(index_at)].set(top_value)


def steps_of(own_key, extent, split, smallest, high):
    loudness, own = 1.0, jax.random.fold_in(own_key, 6)
    for axis_at, blocks in split:
        heights = jnp.exp(jax.random.uniform(jax.random.fold_in(own, axis_at), (blocks,), jnp.float32, smallest / len(split), high / len(split)))
        loudness = loudness * jnp.repeat(heights, extent[axis_at] // blocks).reshape([-1 if axis == axis_at else 1 for axis in range(len(extent))])
    return loudness


def scatter_about(own_key, extent, spread, reach, pieces=(), kind=jnp.bfloat16):
    gain = steps_of(own_key, extent, pieces, -0.22, 0.18) if pieces else 1.0
    array = jax.random.normal(own_key, extent, jnp.float32) * spread * gain
    return jnp.minimum(jnp.maximum(array, -reach), reach).astype(kind)


def setup_inputs(seed: int = 0, part: int = 0) -> dict:
    keys = jax.random.split(jax.random.key(seed), 9)
    part_splits = jax.random.split(jax.random.fold_in(keys[8], part), 9)
    return {
        "data": scatter_about(part_splits[0], (2, NF, SHOTS, RCV), 1.0, 6.0, ((1, 4), (2, 2), (3, 2))),
        "estimate": scatter_about(part_splits[1], (2, NF, ROWS, RCV), RCV ** -0.5, 0.09375, ((1, 4), (2, 2), (3, 2))),
        "window_data": scatter_about(part_splits[2], (2, NF, ROWS, SHOTS), 1.0, 6.0, ((1, 4), (2, 2))),
        "wavelet": scatter_about(part_splits[3], (2, NF), 4.0, 24.0, ((1, 4),), jnp.float32),
        "positions": touch_ends(jax.random.randint(part_splits[4], (SHOTS,), 0, RCV), jax.random.fold_in(part_splits[4], 1), 0, RCV - 1).astype(jnp.int32),
        "bins": touch_ends(jax.random.randint(part_splits[5], (NF,), 0, NBIN), jax.random.fold_in(part_splits[5], 1), 0, NBIN - 1).astype(jnp.int32),
        "threshold": jax.random.randint(part_splits[6], (1,), 8, 41).astype(jnp.int32),
        "step": jnp.clip(jnp.exp(jax.random.uniform(part_splits[7], (1,), jnp.float32, math.log(0.25), math.log(1.0))), 0.25, 1.0),
    }


def reference(data, estimate, window_data, wavelet, positions, bins, threshold, step):
    norm = 1.0 / math.sqrt(SHOTS * RCV)
    step_size = step[0]
    select = (jnp.arange(RCV, dtype=jnp.int32)[None, :] == positions[:, None]).astype(jnp.float32)

    def per_freq(items):
        est_re, est_im, line_re, line_im, rec_re, rec_im, source = items
        down_re = (source[0] * select - line_re.astype(jnp.float32)).astype(jnp.bfloat16)
        down_im = (source[1] * select - line_im.astype(jnp.float32)).astype(jnp.bfloat16)
        model_re = jnp.dot(est_re, down_re.T, preferred_element_type=jnp.float32) - jnp.dot(est_im, down_im.T, preferred_element_type=jnp.float32)
        model_im = jnp.dot(est_re, down_im.T, preferred_element_type=jnp.float32) + jnp.dot(est_im, down_re.T, preferred_element_type=jnp.float32)
        err_re = (rec_re.astype(jnp.float32) - model_re).astype(jnp.bfloat16)
        err_im = (rec_im.astype(jnp.float32) - model_im).astype(jnp.bfloat16)
        grad_re = jnp.dot(err_re, down_re, preferred_element_type=jnp.float32) + jnp.dot(err_im, down_im, preferred_element_type=jnp.float32)
        grad_im = jnp.dot(err_im, down_re, preferred_element_type=jnp.float32) - jnp.dot(err_re, down_im, preferred_element_type=jnp.float32)
        upd_re = (est_re.astype(jnp.float32) - step_size * (grad_re * norm)).astype(jnp.bfloat16)
        upd_im = (est_im.astype(jnp.float32) - step_size * (grad_im * norm)).astype(jnp.bfloat16)
        return (upd_re, upd_im)
    upd_re, upd_im = lax.map(per_freq, (estimate[0], estimate[1], data[0], data[1], window_data[0], window_data[1], wavelet.T))
    times = jnp.arange(NT, dtype=jnp.int32)
    phase = bins[:, None] * times[None, :] % NT
    angle = 2.0 * math.pi / NT * phase.astype(jnp.float32)
    table = jnp.concatenate([jnp.cos(angle), -jnp.sin(angle)], axis=0).astype(jnp.bfloat16)
    stacked = jnp.concatenate([upd_re, upd_im], axis=0).reshape(2 * NF, ROWS * RCV)
    trace = jnp.dot(table.T, stacked, preferred_element_type=jnp.float32) * math.sqrt(RCV / NF)
    trace = trace.reshape(NT, ROWS, RCV)
    level = threshold[0].astype(jnp.float32) / 64.0
    return (jnp.sign(trace) * jnp.maximum(jnp.abs(trace) - level, 0.0)).astype(jnp.bfloat16)
```

```python
from functools import partial
import math

import jax
import jax.numpy as jnp
from jax import lax
from jax.experimental import pallas as pl
from jax.experimental.pallas import tpu as pltpu
from jax.sharding import PartitionSpec as P

NF = 256
RCV = 4096
NT = 1024

OCT = 8
SLAB = 2 * OCT * OCT
LANES = 128
TILE = 256
PARAMS = pltpu.CompilerParams(vmem_limit_bytes=40 * 1024 * 1024)
TIME_PARAMS = pltpu.CompilerParams(vmem_limit_bytes=60 * 1024 * 1024)


def make_down(lines, spots, wavelet, offset):
    width = lines.shape[3]
    columns = offset + lax.iota(jnp.int32, width)
    select = (columns[None, None, :] == spots[None, :, None]).astype(jnp.float32)
    down_re = (wavelet[0][:, None, None] * select - lines[0].astype(jnp.float32)).astype(
        jnp.bfloat16
    )
    down_im = (wavelet[1][:, None, None] * select - lines[1].astype(jnp.float32)).astype(
        jnp.bfloat16
    )
    return (down_re, down_im)


def general_body(data, estimate, window_data, wavelet, positions, bins, threshold, step):
    product = partial(jnp.einsum, preferred_element_type=jnp.float32)
    offset = lax.axis_index("rcv") * data.shape[3]
    shots_all = data.shape[2] * lax.axis_size("shot")
    norm = 1.0 / math.sqrt(shots_all * RCV)
    lines, spots = (
        lax.all_gather(data, "shot", axis=2, tiled=True),
        lax.all_gather(positions, "shot", axis=0, tiled=True),
    )
    down_re, down_im = make_down(lines, spots, wavelet, offset)
    rows_re = estimate[0]
    rows_im = estimate[1]
    model_re = product("frc,fsc->frs", rows_re, down_re) - product("frc,fsc->frs", rows_im, down_im)
    model_im = product("frc,fsc->frs", rows_re, down_im) + product("frc,fsc->frs", rows_im, down_re)
    model_re, model_im = lax.psum((model_re, model_im), "rcv")
    err_re = (window_data[0].astype(jnp.float32) - model_re).astype(jnp.bfloat16)
    err_im = (window_data[1].astype(jnp.float32) - model_im).astype(jnp.bfloat16)
    grad_re = product("frs,fsc->frc", err_re, down_re) + product("frs,fsc->frc", err_im, down_im)
    grad_im = product("frs,fsc->frc", err_im, down_re) - product("frs,fsc->frc", err_re, down_im)
    step_size = step[0]
    upd_re = (estimate[0].astype(jnp.float32) - step_size * (grad_re * norm)).astype(jnp.bfloat16)
    upd_im = (estimate[1].astype(jnp.float32) - step_size * (grad_im * norm)).astype(jnp.bfloat16)
    updated = jnp.stack([upd_re, upd_im], axis=0)
    n_freq = bins.shape[0]
    times = lax.iota(jnp.int32, NT)
    phase = bins[:, None] * times[None, :] % NT
    angle = 2.0 * math.pi / NT * phase.astype(jnp.float32)
    table = jnp.concatenate([jnp.cos(angle), -jnp.sin(angle)], axis=0).astype(jnp.bfloat16)
    level = threshold[0].astype(jnp.float32) / 64.0
    amplitude = math.sqrt(RCV / NF)
    piece = lax.all_to_all(updated, "freq", split_axis=3, concat_axis=1, tiled=True)
    row_count = piece.shape[2]
    col_count = piece.shape[3]
    stacked = piece.reshape(2 * n_freq, row_count * col_count)
    trace = (
        lax.dot_general(
            table, stacked, (((0,), (0,)), ((), ())), preferred_element_type=jnp.float32
        )
        * amplitude
    )
    sparse = (jnp.sign(trace) * jnp.maximum(jnp.abs(trace) - level, 0.0)).astype(jnp.bfloat16)
    sparse = sparse.reshape(NT, row_count, col_count)
    return lax.all_to_all(sparse, "freq", split_axis=0, concat_axis=2, tiled=True)


VMEM = pltpu.VMEM
SMEM = pltpu.SMEM


def whole(space=VMEM):
    return pl.BlockSpec(memory_space=space)


def natural_slab(ref, g):
    width = ref.shape[3]
    return ref[:, pl.ds(g * OCT, OCT)].astype(jnp.float32).reshape(SLAB, width)


def down_kernel(first, data_ref, wave_ref, spot_ref, down_ref):
    width = data_ref.shape[3]
    row = lax.broadcasted_iota(jnp.int32, (OCT, width), 0)
    column = lax.broadcasted_iota(jnp.int32, (OCT, width), 1)
    spot = jnp.full((OCT, width), -1, jnp.int32)
    for shot in range(OCT):
        spot = jnp.where(row == shot, spot_ref[shot], spot)
    select = column == spot
    for g in range(down_ref.shape[0]):
        line = natural_slab(data_ref, g)
        wave = [
            jnp.where(select, wave_ref[part, first + g * OCT + f], 0.0)
            for part in range(2)
            for f in range(OCT)
        ]
        down_ref[g] = (jnp.concatenate(wave, axis=0) - line).astype(jnp.bfloat16)


def one_hot(shape, target):
    r = lax.broadcasted_iota(jnp.int32, shape, 0)
    c = lax.broadcasted_iota(jnp.int32, shape, 1)
    return target(r, c).astype(jnp.bfloat16)


def rows_kernel(side_ref, est_ref, win_ref, down_ref, rows_ref, model_ref, wide_ref):
    order = one_hot(
        (SLAB, SLAB),
        lambda r, c: c
        == ((r // OCT) % 2) * (OCT * OCT) + (r % OCT) * OCT + r // (2 * OCT),
    )
    half = OCT * OCT
    turn = one_hot((half, half), lambda r, c: c == (r % OCT) * OCT + r // OCT)
    for g in range(rows_ref.shape[0]):
        est = natural_slab(est_ref, g).astype(jnp.bfloat16)
        rows = jnp.dot(order, est, preferred_element_type=jnp.float32).astype(jnp.bfloat16)
        rows_ref[g] = rows
        model_ref[g] = lax.dot_general(
            rows, down_ref[g], (((1,), (1,)), ((), ())), preferred_element_type=jnp.float32
        )
        win = natural_slab(win_ref, g).astype(jnp.bfloat16)
        for other in range(2):
            side = side_ref[0] if other == 0 else 1 - side_ref[0]
            total = jnp.zeros((half, LANES), jnp.float32)
            for part in range(2):
                spread = one_hot(
                    (2 * OCT, LANES),
                    lambda r, c: (c // half == part) & (r == side * OCT + c % OCT),
                )
                rows_of = jnp.dot(
                    turn, win[part * half : (part + 1) * half], preferred_element_type=jnp.float32
                )
                total += jnp.dot(
                    rows_of.astype(jnp.bfloat16), spread, preferred_element_type=jnp.float32
                )
            wide_ref[g, other] = total


def lane_sign(rows, low):
    lane = lax.broadcasted_iota(jnp.int32, (rows, LANES), 1)
    return jnp.where(lane < LANES // 2, low, -low)


def complex_model(products):
    half = SLAB // 2
    split = products.reshape(OCT, 2, OCT, LANES)
    first = split[:, 0].reshape(half, LANES)
    second = pltpu.roll(split[:, 1].reshape(half, LANES), LANES // 2, 1)
    return first + lane_sign(half, -1.0) * second


def model_kernel(rows_ref, other_ref, own_model_ref, model_ref):
    for g in range(rows_ref.shape[0]):
        other = lax.dot_general(
            rows_ref[g], other_ref[g], (((1,), (1,)), ((), ())), preferred_element_type=jnp.float32
        )
        model_ref[g, 0] = complex_model(own_model_ref[g])
        model_ref[g, 1] = complex_model(other)


def factors(misfit):
    half = SLAB // 2
    r = lax.broadcasted_iota(jnp.int32, (half, LANES), 0)
    c = lax.broadcasted_iota(jnp.int32, (half, LANES), 1)
    same = r % OCT == (c // OCT) % OCT
    re = jnp.where(same, misfit.astype(jnp.bfloat16).astype(jnp.float32), 0.0)
    im = pltpu.roll(re, LANES // 2, 1) * lane_sign(half, 1.0)
    both = jnp.stack([re.reshape(OCT, OCT, LANES), im.reshape(OCT, OCT, LANES)], axis=1)
    return both.reshape(SLAB, LANES).astype(jnp.bfloat16)


def update_kernel(norm, carried, kept, step_ref, rows_ref, own_ref, other_ref, win_ref, mine_ref, far_ref, *rest):
    outs = rest[carried + kept :]
    step = step_ref[0]
    n = rows_ref.shape[0]
    if carried:
        outs[0][pl.ds(n, n)] = rest[0][...]
    for g in range(n):
        misfit = win_ref[g] - (mine_ref[g] + far_ref[g])
        grad = jnp.dot(factors(misfit[0]), own_ref[g], preferred_element_type=jnp.float32)
        grad += jnp.dot(factors(misfit[1]), other_ref[g], preferred_element_type=jnp.float32)
        updated = (rows_ref[g].astype(jnp.float32) - step * (grad * norm)).astype(jnp.bfloat16)
        at = 0
        for out in outs:
            width = out.shape[2]
            out[g] = updated[:, at : at + width]
            at += width


def time_kernel(plan, blocks, aliased, level_ref, table_ref, *rest):
    n_refs = sum(plan)
    sources = rest[:n_refs]
    rest = rest[n_refs + aliased :]
    outs, scratch = rest[:blocks], rest[blocks]
    level = level_ref[0]
    span = outs[0].shape[0]
    width = outs[0].shape[2]
    for i in range(OCT):
        rows = []
        at = 0
        for n in plan:
            for g in range(sources[at].shape[0]):
                parts = [ref[g, pl.ds(i * 2 * OCT, 2 * OCT), :] for ref in sources[at : at + n]]
                rows.append(sum(parts[1:], parts[0]))
            at += n
        stacked = jnp.concatenate(rows, axis=0)
        trace = jnp.dot(table_ref[...], stacked, preferred_element_type=jnp.float32)
        sparse = trace - jnp.clip(trace, -level, level)
        for b in range(blocks):
            for c in range(width // LANES):
                scratch[b, c, pl.ds(i, span, stride=OCT), :] = sparse[
                    b * span : (b + 1) * span, c * LANES : (c + 1) * LANES
                ]
    for b in range(blocks):
        for c in range(width // LANES):
            outs[b][:, :, pl.ds(c * LANES, LANES)] = (
                scratch[b, c].reshape(span, OCT, LANES).astype(jnp.bfloat16)
            )


def pack_kernel(a_ref, b_ref, out_ref):
    n = a_ref.shape[0]
    out_ref[pl.ds(0, n)] = a_ref[...]
    out_ref[pl.ds(n, n)] = b_ref[...]


def place_kernel(column, outer_ref, got_ref, _, out_ref, held, sem):
    @pl.when(outer_ref[0] == 1)
    def _():
        take = pltpu.make_async_copy(got_ref, held, sem)
        take.start()
        take.wait()
        put = pltpu.make_async_copy(held, out_ref.at[:, :, pl.ds(column, TILE)], sem)
        put.start()
        put.wait()


PAIR = ((0, 1), (1, 0), (2, 3), (3, 2))
INWARD = ((0, 1), (3, 2))
MIDDLE = ((1, 2), (2, 1))
OUTWARD = ((1, 0), (2, 3))
CHUNKS = 4
RAW_TILES = 2


def cost(flops, moved):
    return pl.CostEstimate(flops=0, bytes_accessed=0, transcendentals=0)


def tie(*arrays):
    return lax.optimization_barrier(arrays)


def line_body(data, estimate, window_data, wavelet, positions, bins, threshold, step):
    f32, bf16 = jnp.float32, jnp.bfloat16
    sds = jax.ShapeDtypeStruct
    n_own = data.shape[1]
    width = data.shape[3]
    groups = n_own // OCT
    per = groups // CHUNKS
    tiles = width // TILE
    raw = RAW_TILES * TILE
    early = raw + TILE
    late = tiles - RAW_TILES - 1
    z = lax.axis_index("freq")
    x = lax.axis_index("shot")
    norm = 1.0 / math.sqrt(2 * OCT * RCV)
    n_time = NT // 4
    half = SLAB // 2

    spots = positions - lax.axis_index("rcv") * width
    side = x.astype(jnp.int32).reshape(1)
    low = z < 2
    order = jnp.stack([z, z ^ 1, jnp.where(low, 2, 1), jnp.where(low, 3, 0)])
    ordered = bins.reshape(4, groups * OCT)[order].reshape(4 * groups, 1, OCT)
    t = jnp.concatenate(
        [z * n_time + lax.iota(jnp.int32, n_time), (z ^ 1) * n_time + lax.iota(jnp.int32, n_time)]
    )
    phase = t[:, None, None, None] * ordered[None] % NT
    angle = 2.0 * math.pi / NT * phase.astype(f32)
    table = jnp.concatenate([jnp.cos(angle), -jnp.sin(angle)], axis=2).astype(bf16)
    table = (table * math.sqrt(RCV / NF)).astype(bf16).reshape(2 * n_time, 2 * NF)
    level = threshold.astype(f32) / 64.0
    outer = ((z == 0) | (z == 3)).astype(jnp.int32).reshape(1)

    def still(shape):
        return pl.BlockSpec(shape, lambda n: (0,) * len(shape))

    chunk_block = (2, per * OCT, OCT, width)
    slab = (per, SLAB, width)
    slab_bytes = per * SLAB * width * 2
    downs = [
        pl.pallas_call(
            partial(down_kernel, k * per * OCT),
            grid=(1,),
            in_specs=[
                pl.BlockSpec(chunk_block, lambda n, k=k: (0, k, 0, 0)),
                whole(SMEM),
                whole(SMEM),
            ],
            out_specs=still(slab),
            out_shape=sds(slab, bf16),
            compiler_params=PARAMS,
            cost_estimate=cost(0, 2 * slab_bytes),
            name="down",
        )(data, wavelet, spots)
        for k in range(CHUNKS)
    ]
    swap_shots = lambda a: lax.ppermute(a, "shot", ((0, 1), (1, 0)))
    others = [swap_shots(downs[0]), swap_shots(downs[1]), None, None]
    rows, models, wins = [], [], []
    for k in range(CHUNKS):
        e, m, w = pl.pallas_call(
            rows_kernel,
            grid=(1,),
            in_specs=[
                whole(SMEM),
                pl.BlockSpec(chunk_block, lambda n, k=k: (0, k, 0, 0)),
                pl.BlockSpec((2, per * OCT, OCT, 2 * OCT), lambda n, k=k: (0, k, 0, 0)),
                still(slab),
            ],
            out_specs=[still(slab), still((per, SLAB, LANES)), still((per, 2, half, LANES))],
            out_shape=[
                sds(slab, bf16),
                sds((per, SLAB, LANES), f32),
                sds((per, 2, half, LANES), f32),
            ],
            compiler_params=PARAMS,
            cost_estimate=cost(4 * per * SLAB * SLAB * width, 3 * slab_bytes),
            name="rows",
        )(side, estimate, window_data, downs[k])
        rows.append(e)
        models.append(m)
        wins.append(w)
    others[0], table, *rest = tie(others[0], table, *rows, *models, *wins, *downs)
    rows, models, wins, downs = (rest[n * CHUNKS : (n + 1) * CHUNKS] for n in range(4))

    send = lambda a, pairs: lax.ppermute(a, "freq", pairs)
    cut = lambda a: a[:, :, :raw]
    lates = [None] * late
    packed, swaps, mids = ([None] * CHUNKS for _ in range(3))
    forwards = [None] * (CHUNKS + 2)
    for k in range(CHUNKS):
        if k + 2 < CHUNKS:
            others[k], downs[k + 2] = tie(others[k], downs[k + 2])
            others[k + 2] = swap_shots(downs[k + 2])
        mine = pl.pallas_call(
            model_kernel,
            in_specs=[whole()] * 3,
            out_specs=whole(),
            out_shape=sds((per, 2, half, LANES), f32),
            compiler_params=PARAMS,
            cost_estimate=cost(2 * per * SLAB * SLAB * width, 2 * slab_bytes),
            name="model",
        )(rows[k], others[k], models[k])
        far = lax.ppermute(mine, "rcv", ((0, 1), (1, 0)))
        carried, kept = (0, 0) if k == 0 else (1, late)
        packed[k], *lates = pl.pallas_call(
            partial(update_kernel, norm, carried, kept),
            grid=(1,),
            in_specs=[whole(SMEM), still(slab), still(slab), still(slab)]
            + [still((per, 2, half, LANES))] * 3
            + [still((per, SLAB, early))] * carried
            + [pl.BlockSpec(memory_space=pl.ANY)] * kept,
            out_specs=[still(((1 + carried) * per, SLAB, early))]
            + [pl.BlockSpec((per, SLAB, TILE), lambda n, k=k: (k, 0, 0))] * late,
            out_shape=[sds(((1 + carried) * per, SLAB, early), bf16)]
            + [sds((groups, SLAB, TILE), bf16)] * late,
            input_output_aliases={7 + carried + q: 1 + q for q in range(kept)},
            compiler_params=PARAMS,
            cost_estimate=cost(4 * per * SLAB * SLAB * width, 4 * slab_bytes),
            name="update",
        )(step, rows[k], downs[k], others[k], wins[k], mine, far, *swaps[k - 1 : k], *lates[:kept])
        if k:
            packed[k], mids[k - 1], lates[0] = tie(packed[k], mids[k - 1], lates[0])
        if k >= 2:
            packed[k], forwards[k - 1] = tie(packed[k], forwards[k - 1])
        swaps[k] = send(packed[k][:per], PAIR)
        mids[k] = send(packed[k], MIDDLE)
        if k:
            forwards[k] = send(cut(mids[k - 1]), OUTWARD)

    def time_call(sources, plan, specs, table_rows, out, first, grid, name):
        span = grid * TILE * OCT
        own_block = pl.BlockSpec((n_time, OCT, TILE), lambda c: (0, 0, first + c))
        own_shape = sds((n_time, OCT, width), bf16)
        blocks = table_rows // n_time
        aliased = 0 if out is None else 1
        return pl.pallas_call(
            partial(time_kernel, plan, blocks, aliased),
            grid=(grid,),
            in_specs=[whole(SMEM), pl.BlockSpec((table_rows, 2 * NF), lambda c: (0, 0))]
            + specs
            + [pl.BlockSpec(memory_space=pl.ANY)] * aliased,
            out_specs=[own_block] + [still((n_time, OCT, TILE))] * (blocks - 1),
            out_shape=[own_shape] + [sds((n_time, OCT, TILE), bf16)] * (blocks - 1),
            input_output_aliases={2 + len(specs): 0} if aliased else {},
            scratch_shapes=[VMEM((blocks, TILE // LANES, n_time * OCT, LANES), f32)],
            compiler_params=TIME_PARAMS,
            cost_estimate=cost(2 * table_rows * 2 * NF * span, (2 * NF + table_rows) * span * 2),
            name=name,
        )(level, table, *sources, *([out] * aliased))

    def part(n, c0, grid):
        return pl.BlockSpec((per, SLAB, TILE), lambda c: (n, 0, c0 + c if grid else c0))

    last = CHUNKS - 1

    def chunk_sources(c0, grid):
        own = [(packed[k], part(0, c0, grid)) for k in range(CHUNKS)]
        swap = [(swaps[k], part(0, c0, grid)) for k in range(CHUNKS)]
        mid = [(mids[k], part(0, c0, grid)) for k in range(CHUNKS)]
        cross = [(mids[k + 1], part(1, c0, grid)) for k in range(last)]
        cross.append((cross_last, part(0, c0, grid)))
        return own, swap, mid, cross

    def early_time(out):
        sources = sum(chunk_sources(RAW_TILES, False), [])
        arrays, specs = zip(*sources)
        plan = [1] * len(arrays)
        return time_call(
            arrays, plan, list(specs), 2 * n_time, out, RAW_TILES, 1, "time_early"
        )

    def late_time(q, out):
        sources = [lates[q], swaps_in[q], mids_in[q]]
        specs = [still(a.shape) for a in sources]
        return time_call(
            sources, [1] * 3, specs, 2 * n_time, out, RAW_TILES + 1 + q, 1, "time_late"
        )

    def raw_time(out):
        own, swap, mid, cross = chunk_sources(0, True)
        mid_far = [(forwards[k + 1], part(0, 0, True)) for k in range(CHUNKS)]
        cross_far = [(forwards[k + 2], part(1 if k < last else 0, 0, True)) for k in range(CHUNKS)]
        sources = own + swap
        for near, far in zip(mid + cross, mid_far + cross_far):
            sources = sources + [near, far]
        arrays, specs = zip(*sources)
        plan = [1] * (2 * CHUNKS) + [2] * (2 * CHUNKS)
        return time_call(arrays, plan, list(specs), n_time, out, 0, RAW_TILES, "time_raw")[0]

    def place(j, got, out):
        return pl.pallas_call(
            partial(place_kernel, (RAW_TILES + j) * TILE),
            in_specs=[whole(SMEM), whole(pl.ANY), whole(pl.ANY)],
            out_specs=whole(pl.ANY),
            out_shape=sds((n_time, OCT, width), bf16),
            input_output_aliases={2: 0},
            scratch_shapes=[VMEM((n_time, OCT, TILE), bf16), pltpu.SemaphoreType.DMA(())],
            compiler_params=PARAMS,
            cost_estimate=cost(0, 3 * n_time * OCT * TILE * 2),
            name="place",
        )(outer, got, out)

    def pack(a, b):
        n = a.shape[0]
        return pl.pallas_call(
            pack_kernel,
            grid=(1,),
            in_specs=[still(a.shape)] * 2,
            out_specs=still((2 * n,) + a.shape[1:]),
            out_shape=sds((2 * n,) + a.shape[1:], bf16),
            compiler_params=PARAMS,
            cost_estimate=cost(0, 0),
            name="pack",
        )(a, b)

    ends = [None] * (late + 1)
    swaps_in, mids_in = ([None] * late for _ in range(2))
    swaps_in[0] = send(lates[0], INWARD)
    cross_last = send(swaps[last], MIDDLE)
    mids[last], swaps_in[0], forwards[last], lates[1] = tie(
        mids[last], swaps_in[0], forwards[last], lates[1]
    )
    forwards[CHUNKS] = send(cut(mids[last]), OUTWARD)
    mids_in[0] = send(pack(lates[0], swaps_in[0]), MIDDLE)
    swaps_in[1] = send(lates[1], INWARD)
    cross_last, mids[last] = tie(cross_last, mids[last])
    out, theirs = early_time(None)
    ends[0] = send(theirs, OUTWARD)
    cross_last, out, forwards[CHUNKS] = tie(cross_last, out, forwards[CHUNKS])
    forwards[CHUNKS + 1] = send(cut(cross_last), OUTWARD)
    for q in range(late):
        if q + 1 < late:
            swaps_in[q + 1], out = tie(swaps_in[q + 1], out)
            mids_in[q + 1] = send(pack(lates[q + 1], swaps_in[q + 1]), MIDDLE)
            if q + 2 < late:
                lates[q + 2], swaps_in[q + 1] = tie(lates[q + 2], swaps_in[q + 1])
                swaps_in[q + 2] = send(lates[q + 2], INWARD)
            mids_in[q], swaps_in[q + 1] = tie(mids_in[q], swaps_in[q + 1])
        if q:
            ends[q - 1], mids_in[q] = tie(ends[q - 1], mids_in[q])
            out = place(q - 1, ends[q - 1], out)
        if q == 1:
            out = raw_time(out)
        out, theirs = late_time(q, out)
        ends[q + 1] = send(theirs, OUTWARD)
    for j in range(late - 1, late + 1):
        out = place(j, ends[j], out)
    return out


def solution(mesh):
    line = mesh.shape["freq"] == 4 and mesh.shape["shot"] == 2 and mesh.shape["rcv"] == 2
    return jax.shard_map(
        line_body if line else general_body,
        mesh=mesh,
        in_specs=(
            P(None, "freq", ("grp", "shot"), "rcv"),
            P(None, "freq", ("grp", "shot"), "rcv"),
            P(None, "freq", ("grp", "shot"), None),
            P(None, ("grp", "freq")),
            P(("grp", "shot")),
            P("grp"),
            P("grp"),
            P("grp"),
        ),
        out_specs=P("freq", ("grp", "shot"), "rcv"),
        check_vma=False,
    )
```

```python
from functools import partial
import math

import jax
import jax.numpy as jnp
from jax import lax
from jax.experimental import pallas as pl
from jax.experimental.pallas import tpu as pltpu
from jax.sharding import PartitionSpec as P

NF = 256
RCV = 4096
NT = 1024

OCT = 8
SLAB = 2 * OCT * OCT
LANES = 128
TILE = 256
PARAMS = pltpu.CompilerParams(vmem_limit_bytes=40 * 1024 * 1024)
WIDE_PARAMS = pltpu.CompilerParams(vmem_limit_bytes=60 * 1024 * 1024)


def make_down(lines, spots, wavelet, offset):
    width = lines.shape[3]
    columns = offset + lax.iota(jnp.int32, width)
    select = (columns[None, None, :] == spots[None, :, None]).astype(jnp.float32)
    down_re = (wavelet[0][:, None, None] * select - lines[0].astype(jnp.float32)).astype(
        jnp.bfloat16
    )
    down_im = (wavelet[1][:, None, None] * select - lines[1].astype(jnp.float32)).astype(
        jnp.bfloat16
    )
    return (down_re, down_im)


def general_body(data, estimate, window_data, wavelet, positions, bins, threshold, step):
    product = partial(jnp.einsum, preferred_element_type=jnp.float32)
    offset = lax.axis_index("rcv") * data.shape[3]
    shots_all = data.shape[2] * lax.axis_size("shot")
    norm = 1.0 / math.sqrt(shots_all * RCV)
    lines, spots = (
        lax.all_gather(data, "shot", axis=2, tiled=True),
        lax.all_gather(positions, "shot", axis=0, tiled=True),
    )
    down_re, down_im = make_down(lines, spots, wavelet, offset)
    rows_re = estimate[0]
    rows_im = estimate[1]
    model_re = product("frc,fsc->frs", rows_re, down_re) - product("frc,fsc->frs", rows_im, down_im)
    model_im = product("frc,fsc->frs", rows_re, down_im) + product("frc,fsc->frs", rows_im, down_re)
    model_re, model_im = lax.psum((model_re, model_im), "rcv")
    err_re = (window_data[0].astype(jnp.float32) - model_re).astype(jnp.bfloat16)
    err_im = (window_data[1].astype(jnp.float32) - model_im).astype(jnp.bfloat16)
    grad_re = product("frs,fsc->frc", err_re, down_re) + product("frs,fsc->frc", err_im, down_im)
    grad_im = product("frs,fsc->frc", err_im, down_re) - product("frs,fsc->frc", err_re, down_im)
    step_size = step[0]
    upd_re = (estimate[0].astype(jnp.float32) - step_size * (grad_re * norm)).astype(jnp.bfloat16)
    upd_im = (estimate[1].astype(jnp.float32) - step_size * (grad_im * norm)).astype(jnp.bfloat16)
    updated = jnp.stack([upd_re, upd_im], axis=0)
    n_freq = bins.shape[0]
    times = lax.iota(jnp.int32, NT)
    phase = bins[:, None] * times[None, :] % NT
    angle = 2.0 * math.pi / NT * phase.astype(jnp.float32)
    table = jnp.concatenate([jnp.cos(angle), -jnp.sin(angle)], axis=0).astype(jnp.bfloat16)
    level = threshold[0].astype(jnp.float32) / 64.0
    amplitude = math.sqrt(RCV / NF)
    piece = lax.all_to_all(updated, "freq", split_axis=3, concat_axis=1, tiled=True)
    row_count = piece.shape[2]
    col_count = piece.shape[3]
    stacked = piece.reshape(2 * n_freq, row_count * col_count)
    trace = (
        lax.dot_general(
            table, stacked, (((0,), (0,)), ((), ())), preferred_element_type=jnp.float32
        )
        * amplitude
    )
    sparse = (jnp.sign(trace) * jnp.maximum(jnp.abs(trace) - level, 0.0)).astype(jnp.bfloat16)
    sparse = sparse.reshape(NT, row_count, col_count)
    return lax.all_to_all(sparse, "freq", split_axis=0, concat_axis=2, tiled=True)


VMEM = pltpu.VMEM
SMEM = pltpu.SMEM


def whole(space=VMEM):
    return pl.BlockSpec(memory_space=space)


def natural_slab(ref, g):
    width = ref.shape[3]
    return ref[:, pl.ds(g * OCT, OCT)].astype(jnp.float32).reshape(SLAB, width)


def down_kernel(first, data_ref, wave_ref, spot_ref, down_ref):
    width = data_ref.shape[3]
    row = lax.broadcasted_iota(jnp.int32, (OCT, width), 0)
    column = lax.broadcasted_iota(jnp.int32, (OCT, width), 1)
    spot = jnp.full((OCT, width), -1, jnp.int32)
    for shot in range(OCT):
        spot = jnp.where(row == shot, spot_ref[shot], spot)
    select = column == spot
    at = first + pl.program_id(0) * OCT
    for g in range(down_ref.shape[0]):
        line = natural_slab(data_ref, g)
        wave = [
            jnp.where(select, wave_ref[part, at + g * OCT + f], 0.0)
            for part in range(2)
            for f in range(OCT)
        ]
        down_ref[g] = (jnp.concatenate(wave, axis=0) - line).astype(jnp.bfloat16)


def one_hot(shape, target):
    r = lax.broadcasted_iota(jnp.int32, shape, 0)
    c = lax.broadcasted_iota(jnp.int32, shape, 1)
    return target(r, c).astype(jnp.bfloat16)


def rows_kernel(side_ref, est_ref, win_ref, down_ref, rows_ref, model_ref, wide_ref):
    order = one_hot(
        (SLAB, SLAB),
        lambda r, c: c
        == ((r // OCT) % 2) * (OCT * OCT) + (r % OCT) * OCT + r // (2 * OCT),
    )
    half = OCT * OCT
    turn = one_hot((half, half), lambda r, c: c == (r % OCT) * OCT + r // OCT)
    for g in range(rows_ref.shape[0]):
        est = natural_slab(est_ref, g).astype(jnp.bfloat16)
        rows = jnp.dot(order, est, preferred_element_type=jnp.float32).astype(jnp.bfloat16)
        rows_ref[g] = rows
        model_ref[g] = lax.dot_general(
            rows, down_ref[g], (((1,), (1,)), ((), ())), preferred_element_type=jnp.float32
        )
        win = natural_slab(win_ref, g).astype(jnp.bfloat16)
        for other in range(2):
            side = side_ref[0] if other == 0 else 1 - side_ref[0]
            total = jnp.zeros((half, LANES), jnp.float32)
            for part in range(2):
                spread = one_hot(
                    (2 * OCT, LANES),
                    lambda r, c: (c // half == part) & (r == side * OCT + c % OCT),
                )
                rows_of = jnp.dot(
                    turn, win[part * half : (part + 1) * half], preferred_element_type=jnp.float32
                )
                total += jnp.dot(
                    rows_of.astype(jnp.bfloat16), spread, preferred_element_type=jnp.float32
                )
            wide_ref[g, other] = total


def lane_sign(rows, low):
    lane = lax.broadcasted_iota(jnp.int32, (rows, LANES), 1)
    return jnp.where(lane < LANES // 2, low, -low)


def complex_model(products):
    half = SLAB // 2
    split = products.reshape(OCT, 2, OCT, LANES)
    first = split[:, 0].reshape(half, LANES)
    second = pltpu.roll(split[:, 1].reshape(half, LANES), LANES // 2, 1)
    return first + lane_sign(half, -1.0) * second


def model_kernel(rows_ref, other_ref, own_model_ref, model_ref):
    for g in range(rows_ref.shape[0]):
        other = lax.dot_general(
            rows_ref[g], other_ref[g], (((1,), (1,)), ((), ())), preferred_element_type=jnp.float32
        )
        model_ref[g, 0] = complex_model(own_model_ref[g])
        model_ref[g, 1] = complex_model(other)


def factors(misfit):
    half = SLAB // 2
    r = lax.broadcasted_iota(jnp.int32, (half, LANES), 0)
    c = lax.broadcasted_iota(jnp.int32, (half, LANES), 1)
    same = r % OCT == (c // OCT) % OCT
    re = jnp.where(same, misfit.astype(jnp.bfloat16).astype(jnp.float32), 0.0)
    im = pltpu.roll(re, LANES // 2, 1) * lane_sign(half, 1.0)
    both = jnp.stack([re.reshape(OCT, OCT, LANES), im.reshape(OCT, OCT, LANES)], axis=1)
    return both.reshape(SLAB, LANES).astype(jnp.bfloat16)


def update_kernel(norm, kept, step_ref, rows_ref, own_ref, other_ref, win_ref, mine_ref, far_ref, *rest):
    outs = rest[kept:]
    step = step_ref[0]
    for g in range(rows_ref.shape[0]):
        misfit = win_ref[g] - (mine_ref[g] + far_ref[g])
        grad = jnp.dot(factors(misfit[0]), own_ref[g], preferred_element_type=jnp.float32)
        grad += jnp.dot(factors(misfit[1]), other_ref[g], preferred_element_type=jnp.float32)
        updated = (rows_ref[g].astype(jnp.float32) - step * (grad * norm)).astype(jnp.bfloat16)
        at = 0
        for out in outs:
            width = out.shape[2]
            out[g] = updated[:, at : at + width]
            at += width


def time_kernel(plan, blocks, aliased, level_ref, table_ref, *rest):
    n_refs = sum(plan)
    sources = rest[:n_refs]
    rest = rest[n_refs + aliased :]
    outs, scratch = rest[:blocks], rest[blocks]
    level = level_ref[0]
    span = outs[0].shape[0]
    width = outs[0].shape[2]
    for i in range(OCT):
        rows = []
        at = 0
        for n in plan:
            for g in range(sources[at].shape[0]):
                parts = [ref[g, pl.ds(i * 2 * OCT, 2 * OCT), :] for ref in sources[at : at + n]]
                rows.append(sum(parts[1:], parts[0]))
            at += n
        stacked = jnp.concatenate(rows, axis=0)
        trace = jnp.dot(table_ref[...], stacked, preferred_element_type=jnp.float32)
        sparse = trace - jnp.clip(trace, -level, level)
        for b in range(blocks):
            for c in range(width // LANES):
                scratch[b, c, pl.ds(i, span, stride=OCT), :] = sparse[
                    b * span : (b + 1) * span, c * LANES : (c + 1) * LANES
                ]
    for b in range(blocks):
        for c in range(width // LANES):
            outs[b][:, :, pl.ds(c * LANES, LANES)] = (
                scratch[b, c].reshape(span, OCT, LANES).astype(jnp.bfloat16)
            )


def pack_kernel(a_ref, b_ref, out_ref):
    n = a_ref.shape[0]
    out_ref[pl.ds(0, n)] = a_ref[...]
    out_ref[pl.ds(n, n)] = b_ref[...]


def place_kernel(column, outer_ref, got_ref, _, out_ref, held, sem):
    @pl.when(outer_ref[0] == 1)
    def _():
        take = pltpu.make_async_copy(got_ref, held, sem)
        take.start()
        take.wait()
        put = pltpu.make_async_copy(held, out_ref.at[:, :, pl.ds(column, held.shape[2])], sem)
        put.start()
        put.wait()


PAIR = ((0, 1), (1, 0), (2, 3), (3, 2))
INWARD = ((0, 1), (3, 2))
MIDDLE = ((1, 2), (2, 1))
OUTWARD = ((1, 0), (2, 3))
SIZES = (2, 3, 3)
CHUNKS = len(SIZES)
RAW_TILES = 2


def cost(flops, moved):
    return pl.CostEstimate(flops=0, bytes_accessed=0, transcendentals=0)


def tie(*arrays):
    return lax.optimization_barrier(arrays)


def line_body(data, estimate, window_data, wavelet, positions, bins, threshold, step):
    f32, bf16 = jnp.float32, jnp.bfloat16
    sds = jax.ShapeDtypeStruct
    n_own = data.shape[1]
    width = data.shape[3]
    groups = n_own // OCT
    first_group = [sum(SIZES[:k]) for k in range(CHUNKS)]
    tiles = width // TILE
    raw = RAW_TILES * TILE
    early = raw + TILE
    late_widths = [TILE] * (tiles - RAW_TILES - 2) + [TILE // 2] * 2
    late = len(late_widths)
    late_first = [early + sum(late_widths[:q]) for q in range(late)]
    z = lax.axis_index("freq")
    x = lax.axis_index("shot")
    norm = 1.0 / math.sqrt(2 * OCT * RCV)
    n_time = NT // 4
    half = SLAB // 2

    spots = positions - lax.axis_index("rcv") * width
    side = x.astype(jnp.int32).reshape(1)
    low = z < 2
    order = jnp.stack([z, z ^ 1, jnp.where(low, 2, 1), jnp.where(low, 3, 0)])
    ordered = bins.reshape(4, groups, 1, OCT)[order]
    ordered = jnp.broadcast_to(ordered, (4, groups, 2, OCT)).reshape(1, 2 * NF)
    t = jnp.concatenate(
        [z * n_time + lax.iota(jnp.int32, n_time), (z ^ 1) * n_time + lax.iota(jnp.int32, n_time)]
    )
    angle = 2.0 * math.pi / NT * (t[:, None] * ordered % NT).astype(f32)
    real = (lax.broadcasted_iota(jnp.int32, (1, 2 * NF), 1) // OCT) % 2 == 0
    table = jnp.where(real, jnp.cos(angle), -jnp.sin(angle)).astype(bf16)
    table = (table * math.sqrt(RCV / NF)).astype(bf16)
    level = threshold.astype(f32) / 64.0
    outer = ((z == 0) | (z == 3)).astype(jnp.int32).reshape(1)

    def still(shape):
        return pl.BlockSpec(shape, lambda n: (0,) * len(shape))

    def group(*shape):
        return pl.BlockSpec((1,) + shape, lambda n: (n,) + (0,) * len(shape))

    def kernel(body, sizes, **options):
        return pl.pallas_call(body, grid=(sizes,), cost_estimate=cost(0, 0), **options)

    downs = [
        kernel(
            partial(down_kernel, first_group[k] * OCT),
            SIZES[k],
            in_specs=[
                pl.BlockSpec((2, OCT, OCT, width), lambda n, k=k: (0, first_group[k] + n, 0, 0)),
                whole(SMEM),
                whole(SMEM),
            ],
            out_specs=group(SLAB, width),
            out_shape=sds((SIZES[k], SLAB, width), bf16),
            compiler_params=WIDE_PARAMS,
            name="down",
        )(data, wavelet, spots)
        for k in range(CHUNKS)
    ]
    others = [lax.ppermute(a, "shot", ((0, 1), (1, 0))) for a in downs]
    rows, models, wins = [], [], []
    for k in range(CHUNKS):
        e, m, w = kernel(
            rows_kernel,
            SIZES[k],
            in_specs=[
                whole(SMEM),
                pl.BlockSpec((2, OCT, OCT, width), lambda n, k=k: (0, first_group[k] + n, 0, 0)),
                pl.BlockSpec((2, OCT, OCT, 2 * OCT), lambda n, k=k: (0, first_group[k] + n, 0, 0)),
                group(SLAB, width),
            ],
            out_specs=[group(SLAB, width), group(SLAB, LANES), group(2, half, LANES)],
            out_shape=[
                sds((SIZES[k], SLAB, width), bf16),
                sds((SIZES[k], SLAB, LANES), f32),
                sds((SIZES[k], 2, half, LANES), f32),
            ],
            compiler_params=WIDE_PARAMS,
            name="rows",
        )(side, estimate, window_data, downs[k])
        rows.append(e)
        models.append(m)
        wins.append(w)
    others[0], table, *prepared = tie(others[0], table, *rows[:2], *models[:2], *wins[:2])
    rows[:2], models[:2], wins[:2] = prepared[:2], prepared[2:4], prepared[4:]

    send = lambda a, pairs: lax.ppermute(a, "freq", pairs)
    cut = lambda a: a[:, :, :raw]

    def pack(a, b, columns):
        n = a.shape[0]
        return pl.pallas_call(
            pack_kernel,
            grid=(1,),
            in_specs=[still((n, SLAB, columns))] * 2,
            out_specs=still((2 * n, SLAB, columns)),
            out_shape=sds((2 * n, SLAB, columns), bf16),
            compiler_params=PARAMS,
            cost_estimate=cost(0, 0),
            name="pack",
        )(a, b)

    lates = [None] * late
    earlies, swaps, mids, crosses, near_out, far_out = ([None] * CHUNKS for _ in range(6))
    last = CHUNKS - 1
    for k in range(CHUNKS):
        if k:
            others[k], swaps[k - 1] = tie(others[k], swaps[k - 1])
        mine = kernel(
            model_kernel,
            SIZES[k],
            in_specs=[group(SLAB, width), group(SLAB, width), group(SLAB, LANES)],
            out_specs=group(2, half, LANES),
            out_shape=sds((SIZES[k], 2, half, LANES), f32),
            compiler_params=PARAMS,
            name="model",
        )(rows[k], others[k], models[k])
        far = lax.ppermute(mine, "rcv", ((0, 1), (1, 0)))
        kept = 0 if k == 0 else late
        earlies[k], *lates = kernel(
            partial(update_kernel, norm, kept),
            SIZES[k],
            in_specs=[whole(SMEM)]
            + [group(SLAB, width)] * 3
            + [group(2, half, LANES)] * 3
            + [whole(pl.ANY)] * kept,
            out_specs=[group(SLAB, early)]
            + [
                pl.BlockSpec((1, SLAB, w), lambda n, k=k: (first_group[k] + n, 0, 0))
                for w in late_widths
            ],
            out_shape=[sds((SIZES[k], SLAB, early), bf16)]
            + [sds((groups, SLAB, w), bf16) for w in late_widths],
            input_output_aliases={7 + q: 1 + q for q in range(kept)},
            compiler_params=PARAMS,
            name="update",
        )(step, rows[k], downs[k], others[k], wins[k], mine, far, *lates[:kept])
        if k:
            earlies[k], mids[k - 1], crosses[k - 1] = tie(
                earlies[k], mids[k - 1], crosses[k - 1]
            )
        if k:
            earlies[k], near_out[k - 1] = tie(earlies[k], near_out[k - 1])
        if k >= 2:
            earlies[k], far_out[k - 2] = tie(earlies[k], far_out[k - 2])
        swaps[k] = send(earlies[k], PAIR)
        mids[k] = send(earlies[k], MIDDLE)
        if k:
            far_out[k - 1] = send(cut(crosses[k - 1]), OUTWARD)
        beside = [swaps[k], mids[k], lates[0]]
        if k == 0:
            beside += [rows[2], models[2], wins[2]]
        swaps[k], mids[k], lates[0], *beside = tie(*beside)
        if k == 0:
            rows[2], models[2], wins[2] = beside
        crosses[k] = send(swaps[k], MIDDLE)
        near_out[k] = send(cut(mids[k]), OUTWARD)

    def time_call(sources, plan, specs, table_rows, out, first, grid, name, wide=TILE):
        own_block = pl.BlockSpec((n_time, OCT, wide), lambda c: (0, 0, first // wide + c))
        own_shape = sds((n_time, OCT, width), bf16)
        blocks = table_rows // n_time
        aliased = 0 if out is None else 1
        return pl.pallas_call(
            partial(time_kernel, plan, blocks, aliased),
            grid=(grid,),
            in_specs=[whole(SMEM), pl.BlockSpec((table_rows, 2 * NF), lambda c: (0, 0))]
            + specs
            + [pl.BlockSpec(memory_space=pl.ANY)] * aliased,
            out_specs=[own_block] + [still((n_time, OCT, wide))] * (blocks - 1),
            out_shape=[own_shape] + [sds((n_time, OCT, wide), bf16)] * (blocks - 1),
            input_output_aliases={2 + len(specs): 0} if aliased else {},
            scratch_shapes=[VMEM((blocks, wide // LANES, n_time * OCT, LANES), f32)],
            compiler_params=WIDE_PARAMS,
            cost_estimate=cost(0, 0),
            name=name,
        )(level, table, *sources, *([out] * aliased))

    def part(k, n, c0, grid):
        return pl.BlockSpec((SIZES[k], SLAB, TILE), lambda c: (n, 0, c0 + c if grid else c0))

    def chunk_sources(c0, grid):
        ways = (earlies, swaps, mids, crosses)
        return [[(way[k], part(k, 0, c0, grid)) for k in range(CHUNKS)] for way in ways]

    def early_time(out):
        arrays, specs = zip(*sum(chunk_sources(RAW_TILES, False), []))
        plan = [1] * len(arrays)
        return time_call(
            arrays, plan, list(specs), 2 * n_time, out, raw, 1, "time_early"
        )

    def late_time(q, out):
        sources = [lates[q], swaps_in[q], mids_in[q]]
        specs = [still(a.shape) for a in sources]
        wide = late_widths[q]
        return time_call(
            sources, [1] * 3, specs, 2 * n_time, out, late_first[q], 1, "time_late", wide
        )

    def raw_time(out):
        own, swap, mid, cross = chunk_sources(0, True)
        sources = own + swap
        for way, relayed in ((mid, near_out), (cross, far_out)):
            for k in range(CHUNKS):
                sources = sources + [way[k], (relayed[k], part(k, 0, 0, True))]
        arrays, specs = zip(*sources)
        plan = [1] * (2 * CHUNKS) + [2] * (2 * CHUNKS)
        return time_call(arrays, plan, list(specs), n_time, out, 0, RAW_TILES, "time_raw")[0]

    def place(j, got, out):
        return pl.pallas_call(
            partial(place_kernel, late_first[j - 1] if j else raw),
            in_specs=[whole(SMEM), whole(pl.ANY), whole(pl.ANY)],
            out_specs=whole(pl.ANY),
            out_shape=sds((n_time, OCT, width), bf16),
            input_output_aliases={2: 0},
            scratch_shapes=[VMEM(got.shape, bf16), pltpu.SemaphoreType.DMA(())],
            compiler_params=PARAMS,
            cost_estimate=cost(0, 3 * n_time * OCT * TILE * 2),
            name="place",
        )(outer, got, out)

    ends = [None] * (late + 1)
    swaps_in, mids_in = ([None] * late for _ in range(2))
    swaps_in[0] = send(lates[0], INWARD)
    crosses[last], far_out[last - 1], lates[1] = tie(crosses[last], far_out[last - 1], lates[1])
    far_out[last] = send(cut(crosses[last]), OUTWARD)
    out, theirs = early_time(None)
    theirs, near_out[last], far_out[last] = tie(theirs, near_out[last], far_out[last])
    ends[0] = send(theirs, OUTWARD)
    swaps_in[0], out, lates[1] = tie(swaps_in[0], out, lates[1])
    mids_in[0] = send(pack(lates[0], swaps_in[0], late_widths[0]), MIDDLE)
    swaps_in[1] = send(lates[1], INWARD)
    for q in range(late):
        if q:
            ends[q - 1], out = tie(ends[q - 1], out)
            out = place(q - 1, ends[q - 1], out)
        if q + 1 < late:
            swaps_in[q + 1], out = tie(swaps_in[q + 1], out)
            mids_in[q + 1] = send(pack(lates[q + 1], swaps_in[q + 1], late_widths[q + 1]), MIDDLE)
        if q + 2 < late:
            lates[q + 2], swaps_in[q + 1] = tie(lates[q + 2], swaps_in[q + 1])
            swaps_in[q + 2] = send(lates[q + 2], INWARD)
            mids_in[q], swaps_in[q + 2] = tie(mids_in[q], swaps_in[q + 2])
        if q == 1:
            out = raw_time(out)
        out, theirs = late_time(q, out)
        ends[q + 1] = send(theirs, OUTWARD)
    for j in range(late - 1, late + 1):
        out = place(j, ends[j], out)
    return out


def solution(mesh):
    line = mesh.shape["freq"] == 4 and mesh.shape["shot"] == 2 and mesh.shape["rcv"] == 2
    return jax.shard_map(
        line_body if line else general_body,
        mesh=mesh,
        in_specs=(
            P(None, "freq", ("grp", "shot"), "rcv"),
            P(None, "freq", ("grp", "shot"), "rcv"),
            P(None, "freq", ("grp", "shot"), None),
            P(None, ("grp", "freq")),
            P(("grp", "shot")),
            P("grp"),
            P("grp"),
            P("grp"),
        ),
        out_specs=P("freq", ("grp", "shot"), "rcv"),
        check_vma=False,
    )
```

```python
from functools import partial
import math

import jax
import jax.numpy as jnp
from jax import lax
from jax.experimental import pallas as pl
from jax.experimental.pallas import tpu as pltpu
from jax.sharding import PartitionSpec as P

NF = 256
RCV = 4096
NT = 1024

OCT = 8
SLAB = 2 * OCT * OCT
LANES = 128
TILE = 256
PARAMS = pltpu.CompilerParams(vmem_limit_bytes=40 * 1024 * 1024)
WIDE_PARAMS = pltpu.CompilerParams(vmem_limit_bytes=60 * 1024 * 1024)


def make_down(lines, spots, wavelet, offset):
    width = lines.shape[3]
    columns = offset + lax.iota(jnp.int32, width)
    select = (columns[None, None, :] == spots[None, :, None]).astype(jnp.float32)
    down_re = (wavelet[0][:, None, None] * select - lines[0].astype(jnp.float32)).astype(
        jnp.bfloat16
    )
    down_im = (wavelet[1][:, None, None] * select - lines[1].astype(jnp.float32)).astype(
        jnp.bfloat16
    )
    return (down_re, down_im)


def general_body(data, estimate, window_data, wavelet, positions, bins, threshold, step):
    product = partial(jnp.einsum, preferred_element_type=jnp.float32)
    offset = lax.axis_index("rcv") * data.shape[3]
    shots_all = data.shape[2] * lax.axis_size("shot")
    norm = 1.0 / math.sqrt(shots_all * RCV)
    lines, spots = (
        lax.all_gather(data, "shot", axis=2, tiled=True),
        lax.all_gather(positions, "shot", axis=0, tiled=True),
    )
    down_re, down_im = make_down(lines, spots, wavelet, offset)
    rows_re = estimate[0]
    rows_im = estimate[1]
    model_re = product("frc,fsc->frs", rows_re, down_re) - product("frc,fsc->frs", rows_im, down_im)
    model_im = product("frc,fsc->frs", rows_re, down_im) + product("frc,fsc->frs", rows_im, down_re)
    model_re, model_im = lax.psum((model_re, model_im), "rcv")
    err_re = (window_data[0].astype(jnp.float32) - model_re).astype(jnp.bfloat16)
    err_im = (window_data[1].astype(jnp.float32) - model_im).astype(jnp.bfloat16)
    grad_re = product("frs,fsc->frc", err_re, down_re) + product("frs,fsc->frc", err_im, down_im)
    grad_im = product("frs,fsc->frc", err_im, down_re) - product("frs,fsc->frc", err_re, down_im)
    step_size = step[0]
    upd_re = (estimate[0].astype(jnp.float32) - step_size * (grad_re * norm)).astype(jnp.bfloat16)
    upd_im = (estimate[1].astype(jnp.float32) - step_size * (grad_im * norm)).astype(jnp.bfloat16)
    updated = jnp.stack([upd_re, upd_im], axis=0)
    n_freq = bins.shape[0]
    times = lax.iota(jnp.int32, NT)
    phase = bins[:, None] * times[None, :] % NT
    angle = 2.0 * math.pi / NT * phase.astype(jnp.float32)
    table = jnp.concatenate([jnp.cos(angle), -jnp.sin(angle)], axis=0).astype(jnp.bfloat16)
    level = threshold[0].astype(jnp.float32) / 64.0
    amplitude = math.sqrt(RCV / NF)
    piece = lax.all_to_all(updated, "freq", split_axis=3, concat_axis=1, tiled=True)
    row_count = piece.shape[2]
    col_count = piece.shape[3]
    stacked = piece.reshape(2 * n_freq, row_count * col_count)
    trace = (
        lax.dot_general(
            table, stacked, (((0,), (0,)), ((), ())), preferred_element_type=jnp.float32
        )
        * amplitude
    )
    sparse = (jnp.sign(trace) * jnp.maximum(jnp.abs(trace) - level, 0.0)).astype(jnp.bfloat16)
    sparse = sparse.reshape(NT, row_count, col_count)
    return lax.all_to_all(sparse, "freq", split_axis=0, concat_axis=2, tiled=True)


VMEM = pltpu.VMEM
SMEM = pltpu.SMEM


def whole(space=VMEM):
    return pl.BlockSpec(memory_space=space)


def natural_slab(ref, g):
    width = ref.shape[3]
    return ref[:, pl.ds(g * OCT, OCT)].astype(jnp.float32).reshape(SLAB, width)


def down_kernel(first, data_ref, wave_ref, spot_ref, down_ref):
    width = data_ref.shape[3]
    row = lax.broadcasted_iota(jnp.int32, (OCT, width), 0)
    column = lax.broadcasted_iota(jnp.int32, (OCT, width), 1)
    spot = jnp.full((OCT, width), -1, jnp.int32)
    for shot in range(OCT):
        spot = jnp.where(row == shot, spot_ref[shot], spot)
    select = column == spot
    at = first + pl.program_id(0) * OCT
    for g in range(down_ref.shape[0]):
        line = natural_slab(data_ref, g)
        wave = [
            jnp.where(select, wave_ref[part, at + g * OCT + f], 0.0)
            for part in range(2)
            for f in range(OCT)
        ]
        down_ref[g] = (jnp.concatenate(wave, axis=0) - line).astype(jnp.bfloat16)


def one_hot(shape, target):
    r = lax.broadcasted_iota(jnp.int32, shape, 0)
    c = lax.broadcasted_iota(jnp.int32, shape, 1)
    return target(r, c).astype(jnp.bfloat16)


def rows_kernel(side_ref, est_ref, win_ref, down_ref, rows_ref, model_ref, wide_ref):
    order = one_hot(
        (SLAB, SLAB),
        lambda r, c: c
        == ((r // OCT) % 2) * (OCT * OCT) + (r % OCT) * OCT + r // (2 * OCT),
    )
    half = OCT * OCT
    turn = one_hot((half, half), lambda r, c: c == (r % OCT) * OCT + r // OCT)
    for g in range(rows_ref.shape[0]):
        est = natural_slab(est_ref, g).astype(jnp.bfloat16)
        rows = jnp.dot(order, est, preferred_element_type=jnp.float32).astype(jnp.bfloat16)
        rows_ref[g] = rows
        model_ref[g] = lax.dot_general(
            rows, down_ref[g], (((1,), (1,)), ((), ())), preferred_element_type=jnp.float32
        )
        win = natural_slab(win_ref, g).astype(jnp.bfloat16)
        for other in range(2):
            side = side_ref[0] if other == 0 else 1 - side_ref[0]
            total = jnp.zeros((half, LANES), jnp.float32)
            for part in range(2):
                spread = one_hot(
                    (2 * OCT, LANES),
                    lambda r, c: (c // half == part) & (r == side * OCT + c % OCT),
                )
                rows_of = jnp.dot(
                    turn, win[part * half : (part + 1) * half], preferred_element_type=jnp.float32
                )
                total += jnp.dot(
                    rows_of.astype(jnp.bfloat16), spread, preferred_element_type=jnp.float32
                )
            wide_ref[g, other] = total


def lane_sign(rows, low):
    lane = lax.broadcasted_iota(jnp.int32, (rows, LANES), 1)
    return jnp.where(lane < LANES // 2, low, -low)


def complex_model(products):
    half = SLAB // 2
    split = products.reshape(OCT, 2, OCT, LANES)
    first = split[:, 0].reshape(half, LANES)
    second = pltpu.roll(split[:, 1].reshape(half, LANES), LANES // 2, 1)
    return first + lane_sign(half, -1.0) * second


def model_kernel(rows_ref, other_ref, own_model_ref, model_ref):
    for g in range(rows_ref.shape[0]):
        other = lax.dot_general(
            rows_ref[g], other_ref[g], (((1,), (1,)), ((), ())), preferred_element_type=jnp.float32
        )
        model_ref[g, 0] = complex_model(own_model_ref[g])
        model_ref[g, 1] = complex_model(other)


def factors(misfit):
    half = SLAB // 2
    r = lax.broadcasted_iota(jnp.int32, (half, LANES), 0)
    c = lax.broadcasted_iota(jnp.int32, (half, LANES), 1)
    same = r % OCT == (c // OCT) % OCT
    re = jnp.where(same, misfit.astype(jnp.bfloat16).astype(jnp.float32), 0.0)
    im = pltpu.roll(re, LANES // 2, 1) * lane_sign(half, 1.0)
    both = jnp.stack([re.reshape(OCT, OCT, LANES), im.reshape(OCT, OCT, LANES)], axis=1)
    return both.reshape(SLAB, LANES).astype(jnp.bfloat16)


def update_kernel(norm, kept, step_ref, rows_ref, own_ref, other_ref, win_ref, mine_ref, far_ref, *rest):
    outs = rest[kept:]
    step = step_ref[0]
    for g in range(rows_ref.shape[0]):
        misfit = win_ref[g] - (mine_ref[g] + far_ref[g])
        grad = jnp.dot(factors(misfit[0]), own_ref[g], preferred_element_type=jnp.float32)
        grad += jnp.dot(factors(misfit[1]), other_ref[g], preferred_element_type=jnp.float32)
        updated = (rows_ref[g].astype(jnp.float32) - step * (grad * norm)).astype(jnp.bfloat16)
        at = 0
        for out in outs:
            width = out.shape[2]
            out[g] = updated[:, at : at + width]
            at += width


def time_kernel(plan, blocks, aliased, level_ref, table_ref, *rest):
    n_refs = sum(plan)
    sources = rest[:n_refs]
    rest = rest[n_refs + aliased :]
    outs, scratch = rest[:blocks], rest[blocks]
    level = level_ref[0]
    span = outs[0].shape[0]
    width = outs[0].shape[2]
    for i in range(OCT):
        rows = []
        at = 0
        for n in plan:
            for g in range(sources[at].shape[0]):
                parts = [ref[g, pl.ds(i * 2 * OCT, 2 * OCT), :] for ref in sources[at : at + n]]
                rows.append(sum(parts[1:], parts[0]))
            at += n
        stacked = jnp.concatenate(rows, axis=0)
        trace = jnp.dot(table_ref[...], stacked, preferred_element_type=jnp.float32)
        sparse = trace - jnp.clip(trace, -level, level)
        for b in range(blocks):
            for c in range(width // LANES):
                scratch[b, c, pl.ds(i, span, stride=OCT), :] = sparse[
                    b * span : (b + 1) * span, c * LANES : (c + 1) * LANES
                ]
    for b in range(blocks):
        for c in range(width // LANES):
            outs[b][:, :, pl.ds(c * LANES, LANES)] = (
                scratch[b, c].reshape(span, OCT, LANES).astype(jnp.bfloat16)
            )


def pack_kernel(a_ref, b_ref, out_ref):
    n = a_ref.shape[0]
    out_ref[pl.ds(0, n)] = a_ref[...]
    out_ref[pl.ds(n, n)] = b_ref[...]


def place_kernel(column, outer_ref, got_ref, _, out_ref, held, sem):
    @pl.when(outer_ref[0] == 1)
    def _():
        take = pltpu.make_async_copy(got_ref, held, sem)
        take.start()
        take.wait()
        put = pltpu.make_async_copy(held, out_ref.at[:, :, pl.ds(column, held.shape[2])], sem)
        put.start()
        put.wait()


PAIR = ((0, 1), (1, 0), (2, 3), (3, 2))
INWARD = ((0, 1), (3, 2))
MIDDLE = ((1, 2), (2, 1))
OUTWARD = ((1, 0), (2, 3))
SIZES = (2, 3, 3)
CHUNKS = len(SIZES)
RAW_TILES = 2


def cost(flops, moved):
    return pl.CostEstimate(flops=0, bytes_accessed=0, transcendentals=0)


def tie(*arrays):
    return lax.optimization_barrier(arrays)


def line_body(data, estimate, window_data, wavelet, positions, bins, threshold, step):
    f32, bf16 = jnp.float32, jnp.bfloat16
    sds = jax.ShapeDtypeStruct
    n_own = data.shape[1]
    width = data.shape[3]
    groups = n_own // OCT
    first_group = [sum(SIZES[:k]) for k in range(CHUNKS)]
    tiles = width // TILE
    raw = RAW_TILES * TILE
    early = raw + TILE
    late_widths = [TILE] * (tiles - RAW_TILES - 2) + [TILE // 2] * 2
    late = len(late_widths)
    late_first = [early + sum(late_widths[:q]) for q in range(late)]
    z = lax.axis_index("freq")
    x = lax.axis_index("shot")
    norm = 1.0 / math.sqrt(2 * OCT * RCV)
    n_time = NT // 4
    half = SLAB // 2

    spots = positions - lax.axis_index("rcv") * width
    side = x.astype(jnp.int32).reshape(1)
    low = z < 2
    order = jnp.stack([z, z ^ 1, jnp.where(low, 2, 1), jnp.where(low, 3, 0)])
    ordered = bins.reshape(4, groups, 1, OCT)[order]
    ordered = jnp.broadcast_to(ordered, (4, groups, 2, OCT)).reshape(1, 2 * NF)
    t = jnp.concatenate(
        [z * n_time + lax.iota(jnp.int32, n_time), (z ^ 1) * n_time + lax.iota(jnp.int32, n_time)]
    )
    angle = 2.0 * math.pi / NT * (t[:, None] * ordered % NT).astype(f32)
    real = (lax.broadcasted_iota(jnp.int32, (1, 2 * NF), 1) // OCT) % 2 == 0
    table = jnp.where(real, jnp.cos(angle), -jnp.sin(angle)).astype(bf16)
    table = (table * math.sqrt(RCV / NF)).astype(bf16)
    level = threshold.astype(f32) / 64.0
    outer = ((z == 0) | (z == 3)).astype(jnp.int32).reshape(1)

    def still(shape):
        return pl.BlockSpec(shape, lambda n: (0,) * len(shape))

    def group(*shape):
        return pl.BlockSpec((1,) + shape, lambda n: (n,) + (0,) * len(shape))

    def kernel(body, sizes, **options):
        return pl.pallas_call(body, grid=(sizes,), cost_estimate=cost(0, 0), **options)

    downs = [
        kernel(
            partial(down_kernel, first_group[k] * OCT),
            SIZES[k],
            in_specs=[
                pl.BlockSpec((2, OCT, OCT, width), lambda n, k=k: (0, first_group[k] + n, 0, 0)),
                whole(SMEM),
                whole(SMEM),
            ],
            out_specs=group(SLAB, width),
            out_shape=sds((SIZES[k], SLAB, width), bf16),
            compiler_params=WIDE_PARAMS,
            name="down",
        )(data, wavelet, spots)
        for k in range(CHUNKS)
    ]
    others = [lax.ppermute(a, "shot", ((0, 1), (1, 0))) for a in downs]
    rows, models, wins = [], [], []
    for k in range(CHUNKS):
        e, m, w = kernel(
            rows_kernel,
            SIZES[k],
            in_specs=[
                whole(SMEM),
                pl.BlockSpec((2, OCT, OCT, width), lambda n, k=k: (0, first_group[k] + n, 0, 0)),
                pl.BlockSpec((2, OCT, OCT, 2 * OCT), lambda n, k=k: (0, first_group[k] + n, 0, 0)),
                group(SLAB, width),
            ],
            out_specs=[group(SLAB, width), group(SLAB, LANES), group(2, half, LANES)],
            out_shape=[
                sds((SIZES[k], SLAB, width), bf16),
                sds((SIZES[k], SLAB, LANES), f32),
                sds((SIZES[k], 2, half, LANES), f32),
            ],
            compiler_params=WIDE_PARAMS,
            name="rows",
        )(side, estimate, window_data, downs[k])
        rows.append(e)
        models.append(m)
        wins.append(w)
    others[0], table, *prepared = tie(others[0], table, *rows[:2], *models[:2], *wins[:2])
    rows[:2], models[:2], wins[:2] = prepared[:2], prepared[2:4], prepared[4:]

    send = lambda a, pairs: lax.ppermute(a, "freq", pairs)
    cut = lambda a: a[:, :, :raw]

    def pack(a, b, columns):
        n = a.shape[0]
        return pl.pallas_call(
            pack_kernel,
            grid=(1,),
            in_specs=[still((n, SLAB, columns))] * 2,
            out_specs=still((2 * n, SLAB, columns)),
            out_shape=sds((2 * n, SLAB, columns), bf16),
            compiler_params=PARAMS,
            cost_estimate=cost(0, 0),
            name="pack",
        )(a, b)

    lates = [None] * late
    earlies, swaps, mids, crosses, near_out, far_out = ([None] * CHUNKS for _ in range(6))
    last = CHUNKS - 1
    for k in range(CHUNKS):
        if k:
            others[k], swaps[k - 1] = tie(others[k], swaps[k - 1])
        mine = kernel(
            model_kernel,
            SIZES[k],
            in_specs=[group(SLAB, width), group(SLAB, width), group(SLAB, LANES)],
            out_specs=group(2, half, LANES),
            out_shape=sds((SIZES[k], 2, half, LANES), f32),
            compiler_params=PARAMS,
            name="model",
        )(rows[k], others[k], models[k])
        far = lax.ppermute(mine, "rcv", ((0, 1), (1, 0)))
        kept = 0 if k == 0 else late
        earlies[k], *lates = kernel(
            partial(update_kernel, norm, kept),
            SIZES[k],
            in_specs=[whole(SMEM)]
            + [group(SLAB, width)] * 3
            + [group(2, half, LANES)] * 3
            + [whole(pl.ANY)] * kept,
            out_specs=[group(SLAB, early)]
            + [
                pl.BlockSpec((1, SLAB, w), lambda n, k=k: (first_group[k] + n, 0, 0))
                for w in late_widths
            ],
            out_shape=[sds((SIZES[k], SLAB, early), bf16)]
            + [sds((groups, SLAB, w), bf16) for w in late_widths],
            input_output_aliases={7 + q: 1 + q for q in range(kept)},
            compiler_params=PARAMS,
            name="update",
        )(step, rows[k], downs[k], others[k], wins[k], mine, far, *lates[:kept])
        if k:
            earlies[k], mids[k - 1], crosses[k - 1] = tie(
                earlies[k], mids[k - 1], crosses[k - 1]
            )
        if k:
            earlies[k], near_out[k - 1] = tie(earlies[k], near_out[k - 1])
        if k >= 2:
            earlies[k], far_out[k - 2] = tie(earlies[k], far_out[k - 2])
        swaps[k] = send(earlies[k], PAIR)
        mids[k] = send(earlies[k], MIDDLE)
        if k:
            far_out[k - 1] = send(cut(crosses[k - 1]), OUTWARD)
        beside = [swaps[k], lates[0]]
        if k == 0:
            beside += [rows[2], models[2], wins[2]]
        swaps[k], lates[0], *beside = tie(*beside)
        if k == 0:
            rows[2], models[2], wins[2] = beside
        crosses[k] = send(swaps[k], MIDDLE)
        near_out[k] = send(cut(mids[k]), OUTWARD)

    def time_call(sources, plan, specs, table_rows, out, first, grid, name, wide=TILE):
        own_block = pl.BlockSpec((n_time, OCT, wide), lambda c: (0, 0, first // wide + c))
        own_shape = sds((n_time, OCT, width), bf16)
        blocks = table_rows // n_time
        aliased = 0 if out is None else 1
        return pl.pallas_call(
            partial(time_kernel, plan, blocks, aliased),
            grid=(grid,),
            in_specs=[whole(SMEM), pl.BlockSpec((table_rows, 2 * NF), lambda c: (0, 0))]
            + specs
            + [pl.BlockSpec(memory_space=pl.ANY)] * aliased,
            out_specs=[own_block] + [still((n_time, OCT, wide))] * (blocks - 1),
            out_shape=[own_shape] + [sds((n_time, OCT, wide), bf16)] * (blocks - 1),
            input_output_aliases={2 + len(specs): 0} if aliased else {},
            scratch_shapes=[VMEM((blocks, wide // LANES, n_time * OCT, LANES), f32)],
            compiler_params=WIDE_PARAMS,
            cost_estimate=cost(0, 0),
            name=name,
        )(level, table, *sources, *([out] * aliased))

    def part(k, n, c0, grid):
        return pl.BlockSpec((SIZES[k], SLAB, TILE), lambda c: (n, 0, c0 + c if grid else c0))

    def chunk_sources(c0, grid):
        ways = (earlies, swaps, mids, crosses)
        return [[(way[k], part(k, 0, c0, grid)) for k in range(CHUNKS)] for way in ways]

    def early_time(out):
        arrays, specs = zip(*sum(chunk_sources(RAW_TILES, False), []))
        plan = [1] * len(arrays)
        return time_call(
            arrays, plan, list(specs), 2 * n_time, out, raw, 1, "time_early"
        )

    def late_time(q, out):
        sources = [lates[q], swaps_in[q], mids_in[q]]
        specs = [still(a.shape) for a in sources]
        wide = late_widths[q]
        return time_call(
            sources, [1] * 3, specs, 2 * n_time, out, late_first[q], 1, "time_late", wide
        )

    def raw_time(out):
        own, swap, mid, cross = chunk_sources(0, True)
        sources = own + swap
        for way, relayed in ((mid, near_out), (cross, far_out)):
            for k in range(CHUNKS):
                sources = sources + [way[k], (relayed[k], part(k, 0, 0, True))]
        arrays, specs = zip(*sources)
        plan = [1] * (2 * CHUNKS) + [2] * (2 * CHUNKS)
        return time_call(arrays, plan, list(specs), n_time, out, 0, RAW_TILES, "time_raw")[0]

    def place(j, got, out):
        return pl.pallas_call(
            partial(place_kernel, late_first[j - 1] if j else raw),
            in_specs=[whole(SMEM), whole(pl.ANY), whole(pl.ANY)],
            out_specs=whole(pl.ANY),
            out_shape=sds((n_time, OCT, width), bf16),
            input_output_aliases={2: 0},
            scratch_shapes=[VMEM(got.shape, bf16), pltpu.SemaphoreType.DMA(())],
            compiler_params=PARAMS,
            cost_estimate=cost(0, 3 * n_time * OCT * TILE * 2),
            name="place",
        )(outer, got, out)

    ends = [None] * (late + 1)
    swaps_in, mids_in = ([None] * late for _ in range(2))
    swaps_in[0] = send(lates[0], INWARD)
    crosses[last], far_out[last - 1], lates[1] = tie(crosses[last], far_out[last - 1], lates[1])
    far_out[last] = send(cut(crosses[last]), OUTWARD)
    out, theirs = early_time(None)
    theirs, near_out[last], far_out[last] = tie(theirs, near_out[last], far_out[last])
    ends[0] = send(theirs, OUTWARD)
    swaps_in[0], out, lates[1] = tie(swaps_in[0], out, lates[1])
    mids_in[0] = send(pack(lates[0], swaps_in[0], late_widths[0]), MIDDLE)
    swaps_in[1] = send(lates[1], INWARD)
    for q in range(late):
        if q:
            ends[q - 1], out = tie(ends[q - 1], out)
            out = place(q - 1, ends[q - 1], out)
        if q + 1 < late:
            swaps_in[q + 1], out = tie(swaps_in[q + 1], out)
            mids_in[q + 1] = send(pack(lates[q + 1], swaps_in[q + 1], late_widths[q + 1]), MIDDLE)
        if q + 2 < late:
            lates[q + 2], swaps_in[q + 1] = tie(lates[q + 2], swaps_in[q + 1])
            swaps_in[q + 2] = send(lates[q + 2], INWARD)
            mids_in[q], swaps_in[q + 2] = tie(mids_in[q], swaps_in[q + 2])
        if q == 1:
            out = raw_time(out)
        out, theirs = late_time(q, out)
        ends[q + 1] = send(theirs, OUTWARD)
    for j in range(late - 1, late + 1):
        out = place(j, ends[j], out)
    return out


def solution(mesh):
    line = mesh.shape["freq"] == 4 and mesh.shape["shot"] == 2 and mesh.shape["rcv"] == 2
    return jax.shard_map(
        line_body if line else general_body,
        mesh=mesh,
        in_specs=(
            P(None, "freq", ("grp", "shot"), "rcv"),
            P(None, "freq", ("grp", "shot"), "rcv"),
            P(None, "freq", ("grp", "shot"), None),
            P(None, ("grp", "freq")),
            P(("grp", "shot")),
            P("grp"),
            P("grp"),
            P("grp"),
        ),
        out_specs=P("freq", ("grp", "shot"), "rcv"),
        check_vma=False,
    )
```

```python
from functools import partial
import math

import jax
import jax.numpy as jnp
from jax import lax
from jax.experimental import pallas as pl
from jax.experimental.pallas import tpu as pltpu
from jax.sharding import PartitionSpec as P

NF = 256
RCV = 4096
NT = 1024

OCT = 8
SLAB = 2 * OCT * OCT
LANES = 128
TILE = 256
PARAMS = pltpu.CompilerParams(vmem_limit_bytes=40 * 1024 * 1024)
WIDE_PARAMS = pltpu.CompilerParams(vmem_limit_bytes=60 * 1024 * 1024)


def make_down(lines, spots, wavelet, offset):
    width = lines.shape[3]
    columns = offset + lax.iota(jnp.int32, width)
    select = (columns[None, None, :] == spots[None, :, None]).astype(jnp.float32)
    down_re = (wavelet[0][:, None, None] * select - lines[0].astype(jnp.float32)).astype(
        jnp.bfloat16
    )
    down_im = (wavelet[1][:, None, None] * select - lines[1].astype(jnp.float32)).astype(
        jnp.bfloat16
    )
    return (down_re, down_im)


def general_body(data, estimate, window_data, wavelet, positions, bins, threshold, step):
    product = partial(jnp.einsum, preferred_element_type=jnp.float32)
    offset = lax.axis_index("rcv") * data.shape[3]
    shots_all = data.shape[2] * lax.axis_size("shot")
    norm = 1.0 / math.sqrt(shots_all * RCV)
    lines, spots = (
        lax.all_gather(data, "shot", axis=2, tiled=True),
        lax.all_gather(positions, "shot", axis=0, tiled=True),
    )
    down_re, down_im = make_down(lines, spots, wavelet, offset)
    rows_re = estimate[0]
    rows_im = estimate[1]
    model_re = product("frc,fsc->frs", rows_re, down_re) - product("frc,fsc->frs", rows_im, down_im)
    model_im = product("frc,fsc->frs", rows_re, down_im) + product("frc,fsc->frs", rows_im, down_re)
    model_re, model_im = lax.psum((model_re, model_im), "rcv")
    err_re = (window_data[0].astype(jnp.float32) - model_re).astype(jnp.bfloat16)
    err_im = (window_data[1].astype(jnp.float32) - model_im).astype(jnp.bfloat16)
    grad_re = product("frs,fsc->frc", err_re, down_re) + product("frs,fsc->frc", err_im, down_im)
    grad_im = product("frs,fsc->frc", err_im, down_re) - product("frs,fsc->frc", err_re, down_im)
    step_size = step[0]
    upd_re = (estimate[0].astype(jnp.float32) - step_size * (grad_re * norm)).astype(jnp.bfloat16)
    upd_im = (estimate[1].astype(jnp.float32) - step_size * (grad_im * norm)).astype(jnp.bfloat16)
    updated = jnp.stack([upd_re, upd_im], axis=0)
    n_freq = bins.shape[0]
    times = lax.iota(jnp.int32, NT)
    phase = bins[:, None] * times[None, :] % NT
    angle = 2.0 * math.pi / NT * phase.astype(jnp.float32)
    table = jnp.concatenate([jnp.cos(angle), -jnp.sin(angle)], axis=0).astype(jnp.bfloat16)
    level = threshold[0].astype(jnp.float32) / 64.0
    amplitude = math.sqrt(RCV / NF)
    piece = lax.all_to_all(updated, "freq", split_axis=3, concat_axis=1, tiled=True)
    row_count = piece.shape[2]
    col_count = piece.shape[3]
    stacked = piece.reshape(2 * n_freq, row_count * col_count)
    trace = (
        lax.dot_general(
            table, stacked, (((0,), (0,)), ((), ())), preferred_element_type=jnp.float32
        )
        * amplitude
    )
    sparse = (jnp.sign(trace) * jnp.maximum(jnp.abs(trace) - level, 0.0)).astype(jnp.bfloat16)
    sparse = sparse.reshape(NT, row_count, col_count)
    return lax.all_to_all(sparse, "freq", split_axis=0, concat_axis=2, tiled=True)


VMEM = pltpu.VMEM
SMEM = pltpu.SMEM


def whole(space=VMEM):
    return pl.BlockSpec(memory_space=space)


def natural_slab(ref, g):
    width = ref.shape[3]
    return ref[:, pl.ds(g * OCT, OCT)].astype(jnp.float32).reshape(SLAB, width)


def down_kernel(first, data_ref, wave_ref, spot_ref, down_ref):
    width = data_ref.shape[3]
    row = lax.broadcasted_iota(jnp.int32, (OCT, width), 0)
    column = lax.broadcasted_iota(jnp.int32, (OCT, width), 1)
    spot = jnp.full((OCT, width), -1, jnp.int32)
    for shot in range(OCT):
        spot = jnp.where(row == shot, spot_ref[shot], spot)
    select = column == spot
    at = first + pl.program_id(0) * OCT
    for g in range(down_ref.shape[0]):
        line = natural_slab(data_ref, g)
        wave = [
            jnp.where(select, wave_ref[part, at + g * OCT + f], 0.0)
            for part in range(2)
            for f in range(OCT)
        ]
        down_ref[g] = (jnp.concatenate(wave, axis=0) - line).astype(jnp.bfloat16)


def one_hot(shape, target):
    r = lax.broadcasted_iota(jnp.int32, shape, 0)
    c = lax.broadcasted_iota(jnp.int32, shape, 1)
    return target(r, c).astype(jnp.bfloat16)


def rows_kernel(side_ref, est_ref, win_ref, down_ref, rows_ref, model_ref, wide_ref):
    order = one_hot(
        (SLAB, SLAB),
        lambda r, c: c
        == ((r // OCT) % 2) * (OCT * OCT) + (r % OCT) * OCT + r // (2 * OCT),
    )
    half = OCT * OCT
    turn = one_hot((half, half), lambda r, c: c == (r % OCT) * OCT + r // OCT)
    for g in range(rows_ref.shape[0]):
        est = natural_slab(est_ref, g).astype(jnp.bfloat16)
        rows = jnp.dot(order, est, preferred_element_type=jnp.float32).astype(jnp.bfloat16)
        rows_ref[g] = rows
        model_ref[g] = lax.dot_general(
            rows, down_ref[g], (((1,), (1,)), ((), ())), preferred_element_type=jnp.float32
        )
        win = natural_slab(win_ref, g).astype(jnp.bfloat16)
        for other in range(2):
            side = side_ref[0] if other == 0 else 1 - side_ref[0]
            total = jnp.zeros((half, LANES), jnp.float32)
            for part in range(2):
                spread = one_hot(
                    (2 * OCT, LANES),
                    lambda r, c: (c // half == part) & (r == side * OCT + c % OCT),
                )
                rows_of = jnp.dot(
                    turn, win[part * half : (part + 1) * half], preferred_element_type=jnp.float32
                )
                total += jnp.dot(
                    rows_of.astype(jnp.bfloat16), spread, preferred_element_type=jnp.float32
                )
            wide_ref[g, other] = total


def lane_sign(rows, low):
    lane = lax.broadcasted_iota(jnp.int32, (rows, LANES), 1)
    return jnp.where(lane < LANES // 2, low, -low)


def complex_model(products):
    half = SLAB // 2
    split = products.reshape(OCT, 2, OCT, LANES)
    first = split[:, 0].reshape(half, LANES)
    second = pltpu.roll(split[:, 1].reshape(half, LANES), LANES // 2, 1)
    return first + lane_sign(half, -1.0) * second


def model_kernel(rows_ref, other_ref, own_model_ref, model_ref):
    for g in range(rows_ref.shape[0]):
        other = lax.dot_general(
            rows_ref[g], other_ref[g], (((1,), (1,)), ((), ())), preferred_element_type=jnp.float32
        )
        model_ref[g, 0] = complex_model(own_model_ref[g])
        model_ref[g, 1] = complex_model(other)


def factors(misfit):
    half = SLAB // 2
    r = lax.broadcasted_iota(jnp.int32, (half, LANES), 0)
    c = lax.broadcasted_iota(jnp.int32, (half, LANES), 1)
    same = r % OCT == (c // OCT) % OCT
    re = jnp.where(same, misfit.astype(jnp.bfloat16).astype(jnp.float32), 0.0)
    im = pltpu.roll(re, LANES // 2, 1) * lane_sign(half, 1.0)
    both = jnp.stack([re.reshape(OCT, OCT, LANES), im.reshape(OCT, OCT, LANES)], axis=1)
    return both.reshape(SLAB, LANES).astype(jnp.bfloat16)


def update_kernel(norm, kept, step_ref, rows_ref, own_ref, other_ref, win_ref, mine_ref, far_ref, *rest):
    outs = rest[kept:]
    step = step_ref[0]
    for g in range(rows_ref.shape[0]):
        misfit = win_ref[g] - (mine_ref[g] + far_ref[g])
        grad = jnp.dot(factors(misfit[0]), own_ref[g], preferred_element_type=jnp.float32)
        grad += jnp.dot(factors(misfit[1]), other_ref[g], preferred_element_type=jnp.float32)
        updated = (rows_ref[g].astype(jnp.float32) - step * (grad * norm)).astype(jnp.bfloat16)
        at = 0
        for out in outs:
            width = out.shape[2]
            out[g] = updated[:, at : at + width]
            at += width


def time_kernel(plan, blocks, aliased, level_ref, table_ref, *rest):
    n_refs = sum(plan)
    sources = rest[:n_refs]
    rest = rest[n_refs + aliased :]
    outs, scratch = rest[:blocks], rest[blocks]
    level = level_ref[0]
    span = outs[0].shape[0]
    width = outs[0].shape[2]
    for i in range(OCT):
        rows = []
        at = 0
        for n in plan:
            for g in range(sources[at].shape[0]):
                parts = [ref[g, pl.ds(i * 2 * OCT, 2 * OCT), :] for ref in sources[at : at + n]]
                rows.append(sum(parts[1:], parts[0]))
            at += n
        stacked = jnp.concatenate(rows, axis=0)
        trace = jnp.dot(table_ref[...], stacked, preferred_element_type=jnp.float32)
        sparse = trace - jnp.clip(trace, -level, level)
        for b in range(blocks):
            for c in range(width // LANES):
                scratch[b, c, pl.ds(i, span, stride=OCT), :] = sparse[
                    b * span : (b + 1) * span, c * LANES : (c + 1) * LANES
                ]
    for b in range(blocks):
        for c in range(width // LANES):
            outs[b][:, :, pl.ds(c * LANES, LANES)] = (
                scratch[b, c].reshape(span, OCT, LANES).astype(jnp.bfloat16)
            )


def pack_kernel(a_ref, b_ref, out_ref):
    n = a_ref.shape[0]
    out_ref[pl.ds(0, n)] = a_ref[...]
    out_ref[pl.ds(n, n)] = b_ref[...]


def place_kernel(column, outer_ref, got_ref, _, out_ref, held, sem):
    @pl.when(outer_ref[0] == 1)
    def _():
        take = pltpu.make_async_copy(got_ref, held, sem)
        take.start()
        take.wait()
        put = pltpu.make_async_copy(held, out_ref.at[:, :, pl.ds(column, held.shape[2])], sem)
        put.start()
        put.wait()


PAIR = ((0, 1), (1, 0), (2, 3), (3, 2))
INWARD = ((0, 1), (3, 2))
MIDDLE = ((1, 2), (2, 1))
OUTWARD = ((1, 0), (2, 3))
SIZES = (2, 3, 3)
CHUNKS = len(SIZES)
RAW_TILES = 2


def cost(flops, moved):
    return pl.CostEstimate(flops=0, bytes_accessed=0, transcendentals=0)


def tie(*arrays):
    return lax.optimization_barrier(arrays)


def line_body(data, estimate, window_data, wavelet, positions, bins, threshold, step):
    f32, bf16 = jnp.float32, jnp.bfloat16
    sds = jax.ShapeDtypeStruct
    n_own = data.shape[1]
    width = data.shape[3]
    groups = n_own // OCT
    first_group = [sum(SIZES[:k]) for k in range(CHUNKS)]
    tiles = width // TILE
    raw = RAW_TILES * TILE
    early = raw + TILE
    late_widths = [TILE] * (tiles - RAW_TILES - 2) + [TILE // 2] * 2
    late = len(late_widths)
    late_first = [early + sum(late_widths[:q]) for q in range(late)]
    z = lax.axis_index("freq")
    x = lax.axis_index("shot")
    norm = 1.0 / math.sqrt(2 * OCT * RCV)
    n_time = NT // 4
    half = SLAB // 2

    spots = positions - lax.axis_index("rcv") * width
    side = x.astype(jnp.int32).reshape(1)
    low = z < 2
    order = jnp.stack([z, z ^ 1, jnp.where(low, 2, 1), jnp.where(low, 3, 0)])
    ordered = bins.reshape(4, groups, 1, OCT)[order]
    ordered = jnp.broadcast_to(ordered, (4, groups, 2, OCT)).reshape(1, 2 * NF)
    t = jnp.concatenate(
        [z * n_time + lax.iota(jnp.int32, n_time), (z ^ 1) * n_time + lax.iota(jnp.int32, n_time)]
    )
    angle = 2.0 * math.pi / NT * (t[:, None] * ordered % NT).astype(f32)
    real = (lax.broadcasted_iota(jnp.int32, (1, 2 * NF), 1) // OCT) % 2 == 0
    table = jnp.where(real, jnp.cos(angle), -jnp.sin(angle)).astype(bf16)
    table = (table * math.sqrt(RCV / NF)).astype(bf16)
    level = threshold.astype(f32) / 64.0
    outer = ((z == 0) | (z == 3)).astype(jnp.int32).reshape(1)

    def still(shape):
        return pl.BlockSpec(shape, lambda n: (0,) * len(shape))

    def group(*shape):
        return pl.BlockSpec((1,) + shape, lambda n: (n,) + (0,) * len(shape))

    def kernel(body, sizes, **options):
        return pl.pallas_call(body, grid=(sizes,), cost_estimate=cost(0, 0), **options)

    downs = [
        kernel(
            partial(down_kernel, first_group[k] * OCT),
            SIZES[k],
            in_specs=[
                pl.BlockSpec((2, OCT, OCT, width), lambda n, k=k: (0, first_group[k] + n, 0, 0)),
                whole(SMEM),
                whole(SMEM),
            ],
            out_specs=group(SLAB, width),
            out_shape=sds((SIZES[k], SLAB, width), bf16),
            compiler_params=WIDE_PARAMS,
            name="down",
        )(data, wavelet, spots)
        for k in range(CHUNKS)
    ]
    others = [lax.ppermute(a, "shot", ((0, 1), (1, 0))) for a in downs]
    rows, models, wins = [], [], []
    for k in range(CHUNKS):
        e, m, w = kernel(
            rows_kernel,
            SIZES[k],
            in_specs=[
                whole(SMEM),
                pl.BlockSpec((2, OCT, OCT, width), lambda n, k=k: (0, first_group[k] + n, 0, 0)),
                pl.BlockSpec((2, OCT, OCT, 2 * OCT), lambda n, k=k: (0, first_group[k] + n, 0, 0)),
                group(SLAB, width),
            ],
            out_specs=[group(SLAB, width), group(SLAB, LANES), group(2, half, LANES)],
            out_shape=[
                sds((SIZES[k], SLAB, width), bf16),
                sds((SIZES[k], SLAB, LANES), f32),
                sds((SIZES[k], 2, half, LANES), f32),
            ],
            compiler_params=WIDE_PARAMS,
            name="rows",
        )(side, estimate, window_data, downs[k])
        rows.append(e)
        models.append(m)
        wins.append(w)
    others[0], table, *prepared = tie(others[0], table, *rows[:2], *models[:2], *wins[:2])
    rows[:2], models[:2], wins[:2] = prepared[:2], prepared[2:4], prepared[4:]

    send = lambda a, pairs: lax.ppermute(a, "freq", pairs)
    cut = lambda a: a[:, :, :raw]

    def pack(a, b, columns):
        n = a.shape[0]
        return pl.pallas_call(
            pack_kernel,
            grid=(1,),
            in_specs=[still((n, SLAB, columns))] * 2,
            out_specs=still((2 * n, SLAB, columns)),
            out_shape=sds((2 * n, SLAB, columns), bf16),
            compiler_params=PARAMS,
            cost_estimate=cost(0, 0),
            name="pack",
        )(a, b)

    lates = [None] * late
    earlies, swaps, mids, crosses, near_out, far_out = ([None] * CHUNKS for _ in range(6))
    last = CHUNKS - 1
    for k in range(CHUNKS):
        if k:
            others[k], swaps[k - 1] = tie(others[k], swaps[k - 1])
        mine = kernel(
            model_kernel,
            SIZES[k],
            in_specs=[group(SLAB, width), group(SLAB, width), group(SLAB, LANES)],
            out_specs=group(2, half, LANES),
            out_shape=sds((SIZES[k], 2, half, LANES), f32),
            compiler_params=PARAMS,
            name="model",
        )(rows[k], others[k], models[k])
        far = lax.ppermute(mine, "rcv", ((0, 1), (1, 0)))
        kept = 0 if k == 0 else late
        earlies[k], *lates = kernel(
            partial(update_kernel, norm, kept),
            SIZES[k],
            in_specs=[whole(SMEM)]
            + [group(SLAB, width)] * 3
            + [group(2, half, LANES)] * 3
            + [whole(pl.ANY)] * kept,
            out_specs=[group(SLAB, early)]
            + [
                pl.BlockSpec((1, SLAB, w), lambda n, k=k: (first_group[k] + n, 0, 0))
                for w in late_widths
            ],
            out_shape=[sds((SIZES[k], SLAB, early), bf16)]
            + [sds((groups, SLAB, w), bf16) for w in late_widths],
            input_output_aliases={7 + q: 1 + q for q in range(kept)},
            compiler_params=PARAMS,
            name="update",
        )(step, rows[k], downs[k], others[k], wins[k], mine, far, *lates[:kept])
        if k:
            earlies[k], mids[k - 1], crosses[k - 1] = tie(
                earlies[k], mids[k - 1], crosses[k - 1]
            )
        if k:
            earlies[k], near_out[k - 1] = tie(earlies[k], near_out[k - 1])
        if k >= 2:
            earlies[k], far_out[k - 2] = tie(earlies[k], far_out[k - 2])
        swaps[k] = send(earlies[k], PAIR)
        mids[k] = send(earlies[k], MIDDLE)
        if k:
            far_out[k - 1] = send(cut(crosses[k - 1]), OUTWARD)
        beside = [swaps[k], lates[0]]
        if k == 0:
            beside += [rows[2], models[2], wins[2]]
        swaps[k], lates[0], *beside = tie(*beside)
        if k == 0:
            rows[2], models[2], wins[2] = beside
        crosses[k] = send(swaps[k], MIDDLE)
        near_out[k] = send(cut(mids[k]), OUTWARD)

    def time_call(sources, plan, specs, table_rows, out, first, grid, name, wide=TILE):
        own_block = pl.BlockSpec((n_time, OCT, wide), lambda c: (0, 0, first // wide + c))
        own_shape = sds((n_time, OCT, width), bf16)
        blocks = table_rows // n_time
        aliased = 0 if out is None else 1
        return pl.pallas_call(
            partial(time_kernel, plan, blocks, aliased),
            grid=(grid,),
            in_specs=[whole(SMEM), pl.BlockSpec((table_rows, 2 * NF), lambda c: (0, 0))]
            + specs
            + [pl.BlockSpec(memory_space=pl.ANY)] * aliased,
            out_specs=[own_block] + [still((n_time, OCT, wide))] * (blocks - 1),
            out_shape=[own_shape] + [sds((n_time, OCT, wide), bf16)] * (blocks - 1),
            input_output_aliases={2 + len(specs): 0} if aliased else {},
            scratch_shapes=[VMEM((blocks, wide // LANES, n_time * OCT, LANES), f32)],
            compiler_params=WIDE_PARAMS,
            cost_estimate=cost(0, 0),
            name=name,
        )(level, table, *sources, *([out] * aliased))

    def part(k, n, c0, grid):
        return pl.BlockSpec((SIZES[k], SLAB, TILE), lambda c: (n, 0, c0 + c if grid else c0))

    def chunk_sources(c0, grid):
        ways = (earlies, swaps, mids, crosses)
        return [[(way[k], part(k, 0, c0, grid)) for k in range(CHUNKS)] for way in ways]

    def early_time(out):
        arrays, specs = zip(*sum(chunk_sources(RAW_TILES, False), []))
        plan = [1] * len(arrays)
        theirs = pl.pallas_call(
            partial(time_kernel, plan, 1, 0),
            grid=(1,),
            in_specs=[whole(SMEM), pl.BlockSpec((n_time, 2 * NF), lambda c: (1, 0))] + list(specs),
            out_specs=[still((n_time, OCT, TILE))],
            out_shape=[sds((n_time, OCT, TILE), bf16)],
            scratch_shapes=[VMEM((1, TILE // LANES, n_time * OCT, LANES), f32)],
            compiler_params=WIDE_PARAMS,
            cost_estimate=cost(0, 0),
            name="time_theirs",
        )(level, table, *arrays)[0]
        own = time_call(arrays, plan, list(specs), n_time, out, raw, 1, "time_own")[0]
        return own, theirs

    def late_time(q, out):
        sources = [lates[q], swaps_in[q], mids_in[q]]
        specs = [still(a.shape) for a in sources]
        wide = late_widths[q]
        return time_call(
            sources, [1] * 3, specs, 2 * n_time, out, late_first[q], 1, "time_late", wide
        )

    def raw_time(out):
        own, swap, mid, cross = chunk_sources(0, True)
        sources = own + swap
        for way, relayed in ((mid, near_out), (cross, far_out)):
            for k in range(CHUNKS):
                sources = sources + [way[k], (relayed[k], part(k, 0, 0, True))]
        arrays, specs = zip(*sources)
        plan = [1] * (2 * CHUNKS) + [2] * (2 * CHUNKS)
        return time_call(arrays, plan, list(specs), n_time, out, 0, RAW_TILES, "time_raw")[0]

    def place(j, got, out):
        return pl.pallas_call(
            partial(place_kernel, late_first[j - 1] if j else raw),
            in_specs=[whole(SMEM), whole(pl.ANY), whole(pl.ANY)],
            out_specs=whole(pl.ANY),
            out_shape=sds((n_time, OCT, width), bf16),
            input_output_aliases={2: 0},
            scratch_shapes=[VMEM(got.shape, bf16), pltpu.SemaphoreType.DMA(())],
            compiler_params=PARAMS,
            cost_estimate=cost(0, 3 * n_time * OCT * TILE * 2),
            name="place",
        )(outer, got, out)

    ends = [None] * (late + 1)
    swaps_in, mids_in = ([None] * late for _ in range(2))
    swaps_in[0] = send(lates[0], INWARD)
    crosses[last], far_out[last - 1], lates[1] = tie(crosses[last], far_out[last - 1], lates[1])
    far_out[last] = send(cut(crosses[last]), OUTWARD)
    out, theirs = early_time(None)
    swaps_in[0], theirs, lates[1] = tie(swaps_in[0], theirs, lates[1])
    theirs, near_out[last], far_out[last] = tie(theirs, near_out[last], far_out[last])
    ends[0] = send(theirs, OUTWARD)
    mids_in[0] = send(pack(lates[0], swaps_in[0], late_widths[0]), MIDDLE)
    swaps_in[1] = send(lates[1], INWARD)
    for q in range(late):
        if q:
            ends[q - 1], out = tie(ends[q - 1], out)
            out = place(q - 1, ends[q - 1], out)
        if q + 1 < late:
            swaps_in[q + 1], out = tie(swaps_in[q + 1], out)
            mids_in[q + 1] = send(pack(lates[q + 1], swaps_in[q + 1], late_widths[q + 1]), MIDDLE)
        if q + 2 < late:
            lates[q + 2], swaps_in[q + 1] = tie(lates[q + 2], swaps_in[q + 1])
            swaps_in[q + 2] = send(lates[q + 2], INWARD)
            mids_in[q], swaps_in[q + 2] = tie(mids_in[q], swaps_in[q + 2])
        if q == 1:
            out = raw_time(out)
        out, theirs = late_time(q, out)
        ends[q + 1] = send(theirs, OUTWARD)
    for j in range(late - 1, late + 1):
        out = place(j, ends[j], out)
    return out


def solution(mesh):
    line = mesh.shape["freq"] == 4 and mesh.shape["shot"] == 2 and mesh.shape["rcv"] == 2
    return jax.shard_map(
        line_body if line else general_body,
        mesh=mesh,
        in_specs=(
            P(None, "freq", ("grp", "shot"), "rcv"),
            P(None, "freq", ("grp", "shot"), "rcv"),
            P(None, "freq", ("grp", "shot"), None),
            P(None, ("grp", "freq")),
            P(("grp", "shot")),
            P("grp"),
            P("grp"),
            P("grp"),
        ),
        out_specs=P("freq", ("grp", "shot"), "rcv"),
        check_vma=False,
    )
```

```python
from functools import partial
import math

import jax
import jax.numpy as jnp
from jax import lax
from jax.experimental import pallas as pl
from jax.experimental.pallas import tpu as pltpu
from jax.sharding import PartitionSpec as P

NF = 256
RCV = 4096
NT = 1024

OCT = 8
SLAB = 2 * OCT * OCT
LANES = 128
TILE = 256
PARAMS = pltpu.CompilerParams(vmem_limit_bytes=40 * 1024 * 1024)
WIDE_PARAMS = pltpu.CompilerParams(vmem_limit_bytes=60 * 1024 * 1024)


def make_down(lines, spots, wavelet, offset):
    width = lines.shape[3]
    columns = offset + lax.iota(jnp.int32, width)
    select = (columns[None, None, :] == spots[None, :, None]).astype(jnp.float32)
    down_re = (wavelet[0][:, None, None] * select - lines[0].astype(jnp.float32)).astype(
        jnp.bfloat16
    )
    down_im = (wavelet[1][:, None, None] * select - lines[1].astype(jnp.float32)).astype(
        jnp.bfloat16
    )
    return (down_re, down_im)


def general_body(data, estimate, window_data, wavelet, positions, bins, threshold, step):
    product = partial(jnp.einsum, preferred_element_type=jnp.float32)
    offset = lax.axis_index("rcv") * data.shape[3]
    shots_all = data.shape[2] * lax.axis_size("shot")
    norm = 1.0 / math.sqrt(shots_all * RCV)
    lines, spots = (
        lax.all_gather(data, "shot", axis=2, tiled=True),
        lax.all_gather(positions, "shot", axis=0, tiled=True),
    )
    down_re, down_im = make_down(lines, spots, wavelet, offset)
    rows_re = estimate[0]
    rows_im = estimate[1]
    model_re = product("frc,fsc->frs", rows_re, down_re) - product("frc,fsc->frs", rows_im, down_im)
    model_im = product("frc,fsc->frs", rows_re, down_im) + product("frc,fsc->frs", rows_im, down_re)
    model_re, model_im = lax.psum((model_re, model_im), "rcv")
    err_re = (window_data[0].astype(jnp.float32) - model_re).astype(jnp.bfloat16)
    err_im = (window_data[1].astype(jnp.float32) - model_im).astype(jnp.bfloat16)
    grad_re = product("frs,fsc->frc", err_re, down_re) + product("frs,fsc->frc", err_im, down_im)
    grad_im = product("frs,fsc->frc", err_im, down_re) - product("frs,fsc->frc", err_re, down_im)
    step_size = step[0]
    upd_re = (estimate[0].astype(jnp.float32) - step_size * (grad_re * norm)).astype(jnp.bfloat16)
    upd_im = (estimate[1].astype(jnp.float32) - step_size * (grad_im * norm)).astype(jnp.bfloat16)
    updated = jnp.stack([upd_re, upd_im], axis=0)
    n_freq = bins.shape[0]
    times = lax.iota(jnp.int32, NT)
    phase = bins[:, None] * times[None, :] % NT
    angle = 2.0 * math.pi / NT * phase.astype(jnp.float32)
    table = jnp.concatenate([jnp.cos(angle), -jnp.sin(angle)], axis=0).astype(jnp.bfloat16)
    level = threshold[0].astype(jnp.float32) / 64.0
    amplitude = math.sqrt(RCV / NF)
    piece = lax.all_to_all(updated, "freq", split_axis=3, concat_axis=1, tiled=True)
    row_count = piece.shape[2]
    col_count = piece.shape[3]
    stacked = piece.reshape(2 * n_freq, row_count * col_count)
    trace = (
        lax.dot_general(
            table, stacked, (((0,), (0,)), ((), ())), preferred_element_type=jnp.float32
        )
        * amplitude
    )
    sparse = (jnp.sign(trace) * jnp.maximum(jnp.abs(trace) - level, 0.0)).astype(jnp.bfloat16)
    sparse = sparse.reshape(NT, row_count, col_count)
    return lax.all_to_all(sparse, "freq", split_axis=0, concat_axis=2, tiled=True)


VMEM = pltpu.VMEM
SMEM = pltpu.SMEM


def whole(space=VMEM):
    return pl.BlockSpec(memory_space=space)


def natural_slab(ref, g):
    width = ref.shape[3]
    return ref[:, pl.ds(g * OCT, OCT)].astype(jnp.float32).reshape(SLAB, width)


def down_kernel(first, data_ref, wave_ref, spot_ref, down_ref):
    width = data_ref.shape[3]
    row = lax.broadcasted_iota(jnp.int32, (OCT, width), 0)
    column = lax.broadcasted_iota(jnp.int32, (OCT, width), 1)
    spot = jnp.full((OCT, width), -1, jnp.int32)
    for shot in range(OCT):
        spot = jnp.where(row == shot, spot_ref[shot], spot)
    select = column == spot
    at = first + pl.program_id(0) * OCT
    for g in range(down_ref.shape[0]):
        line = natural_slab(data_ref, g)
        wave = [
            jnp.where(select, wave_ref[part, at + g * OCT + f], 0.0)
            for part in range(2)
            for f in range(OCT)
        ]
        down_ref[g] = (jnp.concatenate(wave, axis=0) - line).astype(jnp.bfloat16)


def one_hot(shape, target):
    r = lax.broadcasted_iota(jnp.int32, shape, 0)
    c = lax.broadcasted_iota(jnp.int32, shape, 1)
    return target(r, c).astype(jnp.bfloat16)


def rows_kernel(side_ref, est_ref, win_ref, down_ref, rows_ref, model_ref, wide_ref):
    order = one_hot(
        (SLAB, SLAB),
        lambda r, c: c
        == ((r // OCT) % 2) * (OCT * OCT) + (r % OCT) * OCT + r // (2 * OCT),
    )
    half = OCT * OCT
    turn = one_hot((half, half), lambda r, c: c == (r % OCT) * OCT + r // OCT)
    for g in range(rows_ref.shape[0]):
        est = natural_slab(est_ref, g).astype(jnp.bfloat16)
        rows = jnp.dot(order, est, preferred_element_type=jnp.float32).astype(jnp.bfloat16)
        rows_ref[g] = rows
        model_ref[g] = lax.dot_general(
            rows, down_ref[g], (((1,), (1,)), ((), ())), preferred_element_type=jnp.float32
        )
        win = natural_slab(win_ref, g).astype(jnp.bfloat16)
        for other in range(2):
            side = side_ref[0] if other == 0 else 1 - side_ref[0]
            total = jnp.zeros((half, LANES), jnp.float32)
            for part in range(2):
                spread = one_hot(
                    (2 * OCT, LANES),
                    lambda r, c: (c // half == part) & (r == side * OCT + c % OCT),
                )
                rows_of = jnp.dot(
                    turn, win[part * half : (part + 1) * half], preferred_element_type=jnp.float32
                )
                total += jnp.dot(
                    rows_of.astype(jnp.bfloat16), spread, preferred_element_type=jnp.float32
                )
            wide_ref[g, other] = total


def lane_sign(rows, low):
    lane = lax.broadcasted_iota(jnp.int32, (rows, LANES), 1)
    return jnp.where(lane < LANES // 2, low, -low)


def complex_model(products):
    half = SLAB // 2
    split = products.reshape(OCT, 2, OCT, LANES)
    first = split[:, 0].reshape(half, LANES)
    second = pltpu.roll(split[:, 1].reshape(half, LANES), LANES // 2, 1)
    return first + lane_sign(half, -1.0) * second


def model_kernel(rows_ref, other_ref, own_model_ref, model_ref):
    for g in range(rows_ref.shape[0]):
        other = lax.dot_general(
            rows_ref[g], other_ref[g], (((1,), (1,)), ((), ())), preferred_element_type=jnp.float32
        )
        model_ref[g, 0] = complex_model(own_model_ref[g])
        model_ref[g, 1] = complex_model(other)


def factors(misfit):
    half = SLAB // 2
    r = lax.broadcasted_iota(jnp.int32, (half, LANES), 0)
    c = lax.broadcasted_iota(jnp.int32, (half, LANES), 1)
    same = r % OCT == (c // OCT) % OCT
    re = jnp.where(same, misfit.astype(jnp.bfloat16).astype(jnp.float32), 0.0)
    im = pltpu.roll(re, LANES // 2, 1) * lane_sign(half, 1.0)
    both = jnp.stack([re.reshape(OCT, OCT, LANES), im.reshape(OCT, OCT, LANES)], axis=1)
    return both.reshape(SLAB, LANES).astype(jnp.bfloat16)


def update_kernel(norm, kept, step_ref, rows_ref, own_ref, other_ref, win_ref, mine_ref, far_ref, *rest):
    outs = rest[kept:]
    step = step_ref[0]
    for g in range(rows_ref.shape[0]):
        misfit = win_ref[g] - (mine_ref[g] + far_ref[g])
        grad = jnp.dot(factors(misfit[0]), own_ref[g], preferred_element_type=jnp.float32)
        grad += jnp.dot(factors(misfit[1]), other_ref[g], preferred_element_type=jnp.float32)
        updated = (rows_ref[g].astype(jnp.float32) - step * (grad * norm)).astype(jnp.bfloat16)
        at = 0
        for out in outs:
            width = out.shape[2]
            out[g] = updated[:, at : at + width]
            at += width


def time_kernel(plan, blocks, aliased, level_ref, table_ref, *rest):
    n_refs = sum(plan)
    sources = rest[:n_refs]
    rest = rest[n_refs + aliased :]
    outs, scratch = rest[:blocks], rest[blocks]
    level = level_ref[0]
    span = outs[0].shape[0]
    width = outs[0].shape[2]
    for i in range(OCT):
        rows = []
        at = 0
        for n in plan:
            for g in range(sources[at].shape[0]):
                parts = [ref[g, pl.ds(i * 2 * OCT, 2 * OCT), :] for ref in sources[at : at + n]]
                rows.append(sum(parts[1:], parts[0]))
            at += n
        stacked = jnp.concatenate(rows, axis=0)
        trace = jnp.dot(table_ref[...], stacked, preferred_element_type=jnp.float32)
        sparse = trace - jnp.clip(trace, -level, level)
        for b in range(blocks):
            for c in range(width // LANES):
                scratch[b, c, pl.ds(i, span, stride=OCT), :] = sparse[
                    b * span : (b + 1) * span, c * LANES : (c + 1) * LANES
                ]
    for b in range(blocks):
        for c in range(width // LANES):
            outs[b][:, :, pl.ds(c * LANES, LANES)] = (
                scratch[b, c].reshape(span, OCT, LANES).astype(jnp.bfloat16)
            )


def pack_kernel(a_ref, b_ref, out_ref):
    n = a_ref.shape[0]
    out_ref[pl.ds(0, n)] = a_ref[...]
    out_ref[pl.ds(n, n)] = b_ref[...]


def place_kernel(column, outer_ref, got_ref, _, out_ref, held, sem):
    @pl.when(outer_ref[0] == 1)
    def _():
        take = pltpu.make_async_copy(got_ref, held, sem)
        take.start()
        take.wait()
        put = pltpu.make_async_copy(held, out_ref.at[:, :, pl.ds(column, held.shape[2])], sem)
        put.start()
        put.wait()


PAIR = ((0, 1), (1, 0), (2, 3), (3, 2))
INWARD = ((0, 1), (3, 2))
MIDDLE = ((1, 2), (2, 1))
OUTWARD = ((1, 0), (2, 3))
SIZES = (2, 3, 3)
CHUNKS = len(SIZES)
RAW_TILES = 2


def cost(flops, moved):
    return pl.CostEstimate(flops=0, bytes_accessed=0, transcendentals=0)


def tie(*arrays):
    return lax.optimization_barrier(arrays)


def line_body(data, estimate, window_data, wavelet, positions, bins, threshold, step):
    f32, bf16 = jnp.float32, jnp.bfloat16
    sds = jax.ShapeDtypeStruct
    n_own = data.shape[1]
    width = data.shape[3]
    groups = n_own // OCT
    first_group = [sum(SIZES[:k]) for k in range(CHUNKS)]
    tiles = width // TILE
    raw = RAW_TILES * TILE
    early = raw + TILE
    late_widths = [TILE] * (tiles - RAW_TILES - 1)
    late = len(late_widths)
    late_first = [early + sum(late_widths[:q]) for q in range(late)]
    z = lax.axis_index("freq")
    x = lax.axis_index("shot")
    norm = 1.0 / math.sqrt(2 * OCT * RCV)
    n_time = NT // 4
    half = SLAB // 2

    spots = positions - lax.axis_index("rcv") * width
    side = x.astype(jnp.int32).reshape(1)
    low = z < 2
    order = jnp.stack([z, z ^ 1, jnp.where(low, 2, 1), jnp.where(low, 3, 0)])
    ordered = bins.reshape(4, groups, 1, OCT)[order]
    ordered = jnp.broadcast_to(ordered, (4, groups, 2, OCT)).reshape(1, 2 * NF)
    t = jnp.concatenate(
        [z * n_time + lax.iota(jnp.int32, n_time), (z ^ 1) * n_time + lax.iota(jnp.int32, n_time)]
    )
    angle = 2.0 * math.pi / NT * (t[:, None] * ordered % NT).astype(f32)
    real = (lax.broadcasted_iota(jnp.int32, (1, 2 * NF), 1) // OCT) % 2 == 0
    table = jnp.where(real, jnp.cos(angle), -jnp.sin(angle)).astype(bf16)
    table = (table * math.sqrt(RCV / NF)).astype(bf16)
    level = threshold.astype(f32) / 64.0
    outer = ((z == 0) | (z == 3)).astype(jnp.int32).reshape(1)

    def still(shape):
        return pl.BlockSpec(shape, lambda n: (0,) * len(shape))

    def group(*shape):
        return pl.BlockSpec((1,) + shape, lambda n: (n,) + (0,) * len(shape))

    def kernel(body, sizes, **options):
        return pl.pallas_call(body, grid=(sizes,), cost_estimate=cost(0, 0), **options)

    downs = [
        kernel(
            partial(down_kernel, first_group[k] * OCT),
            SIZES[k],
            in_specs=[
                pl.BlockSpec((2, OCT, OCT, width), lambda n, k=k: (0, first_group[k] + n, 0, 0)),
                whole(SMEM),
                whole(SMEM),
            ],
            out_specs=group(SLAB, width),
            out_shape=sds((SIZES[k], SLAB, width), bf16),
            compiler_params=WIDE_PARAMS,
            name="down",
        )(data, wavelet, spots)
        for k in range(CHUNKS)
    ]
    others = [lax.ppermute(a, "shot", ((0, 1), (1, 0))) for a in downs]
    rows, models, wins = [], [], []
    for k in range(CHUNKS):
        e, m, w = kernel(
            rows_kernel,
            SIZES[k],
            in_specs=[
                whole(SMEM),
                pl.BlockSpec((2, OCT, OCT, width), lambda n, k=k: (0, first_group[k] + n, 0, 0)),
                pl.BlockSpec((2, OCT, OCT, 2 * OCT), lambda n, k=k: (0, first_group[k] + n, 0, 0)),
                group(SLAB, width),
            ],
            out_specs=[group(SLAB, width), group(SLAB, LANES), group(2, half, LANES)],
            out_shape=[
                sds((SIZES[k], SLAB, width), bf16),
                sds((SIZES[k], SLAB, LANES), f32),
                sds((SIZES[k], 2, half, LANES), f32),
            ],
            compiler_params=WIDE_PARAMS,
            name="rows",
        )(side, estimate, window_data, downs[k])
        rows.append(e)
        models.append(m)
        wins.append(w)
    others[0], table, *prepared = tie(others[0], table, *rows[:2], *models[:2], *wins[:2])
    rows[:2], models[:2], wins[:2] = prepared[:2], prepared[2:4], prepared[4:]

    send = lambda a, pairs: lax.ppermute(a, "freq", pairs)
    cut = lambda a: a[:, :, :raw]

    def pack(a, b, columns):
        n = a.shape[0]
        return pl.pallas_call(
            pack_kernel,
            grid=(1,),
            in_specs=[still((n, SLAB, columns))] * 2,
            out_specs=still((2 * n, SLAB, columns)),
            out_shape=sds((2 * n, SLAB, columns), bf16),
            compiler_params=PARAMS,
            cost_estimate=cost(0, 0),
            name="pack",
        )(a, b)

    lates = [None] * late
    earlies, swaps, mids, crosses, near_out, far_out = ([None] * CHUNKS for _ in range(6))
    last = CHUNKS - 1
    for k in range(CHUNKS):
        if k:
            others[k], swaps[k - 1] = tie(others[k], swaps[k - 1])
        mine = kernel(
            model_kernel,
            SIZES[k],
            in_specs=[group(SLAB, width), group(SLAB, width), group(SLAB, LANES)],
            out_specs=group(2, half, LANES),
            out_shape=sds((SIZES[k], 2, half, LANES), f32),
            compiler_params=PARAMS,
            name="model",
        )(rows[k], others[k], models[k])
        far = lax.ppermute(mine, "rcv", ((0, 1), (1, 0)))
        kept = 0 if k == 0 else late
        earlies[k], *lates = kernel(
            partial(update_kernel, norm, kept),
            SIZES[k],
            in_specs=[whole(SMEM)]
            + [group(SLAB, width)] * 3
            + [group(2, half, LANES)] * 3
            + [whole(pl.ANY)] * kept,
            out_specs=[group(SLAB, early)]
            + [
                pl.BlockSpec((1, SLAB, w), lambda n, k=k: (first_group[k] + n, 0, 0))
                for w in late_widths
            ],
            out_shape=[sds((SIZES[k], SLAB, early), bf16)]
            + [sds((groups, SLAB, w), bf16) for w in late_widths],
            input_output_aliases={7 + q: 1 + q for q in range(kept)},
            compiler_params=PARAMS,
            name="update",
        )(step, rows[k], downs[k], others[k], wins[k], mine, far, *lates[:kept])
        if k:
            earlies[k], mids[k - 1], crosses[k - 1] = tie(
                earlies[k], mids[k - 1], crosses[k - 1]
            )
        if k:
            earlies[k], near_out[k - 1] = tie(earlies[k], near_out[k - 1])
        if k >= 2:
            earlies[k], far_out[k - 2] = tie(earlies[k], far_out[k - 2])
        swaps[k] = send(earlies[k], PAIR)
        mids[k] = send(earlies[k], MIDDLE)
        if k:
            far_out[k - 1] = send(cut(crosses[k - 1]), OUTWARD)
        beside = [swaps[k], lates[0]]
        if k == 0:
            beside += [rows[2], models[2], wins[2]]
        swaps[k], lates[0], *beside = tie(*beside)
        if k == 0:
            rows[2], models[2], wins[2] = beside
        crosses[k] = send(swaps[k], MIDDLE)
        near_out[k] = send(cut(mids[k]), OUTWARD)

    def time_call(sources, plan, specs, table_rows, out, first, grid, name, wide=TILE):
        own_block = pl.BlockSpec((n_time, OCT, wide), lambda c: (0, 0, first // wide + c))
        own_shape = sds((n_time, OCT, width), bf16)
        blocks = table_rows // n_time
        aliased = 0 if out is None else 1
        return pl.pallas_call(
            partial(time_kernel, plan, blocks, aliased),
            grid=(grid,),
            in_specs=[whole(SMEM), pl.BlockSpec((table_rows, 2 * NF), lambda c: (0, 0))]
            + specs
            + [pl.BlockSpec(memory_space=pl.ANY)] * aliased,
            out_specs=[own_block] + [still((n_time, OCT, wide))] * (blocks - 1),
            out_shape=[own_shape] + [sds((n_time, OCT, wide), bf16)] * (blocks - 1),
            input_output_aliases={2 + len(specs): 0} if aliased else {},
            scratch_shapes=[VMEM((blocks, wide // LANES, n_time * OCT, LANES), f32)],
            compiler_params=WIDE_PARAMS,
            cost_estimate=cost(0, 0),
            name=name,
        )(level, table, *sources, *([out] * aliased))

    def part(k, n, c0, grid):
        return pl.BlockSpec((SIZES[k], SLAB, TILE), lambda c: (n, 0, c0 + c if grid else c0))

    def chunk_sources(c0, grid):
        ways = (earlies, swaps, mids, crosses)
        return [[(way[k], part(k, 0, c0, grid)) for k in range(CHUNKS)] for way in ways]

    def early_time(out):
        arrays, specs = zip(*sum(chunk_sources(RAW_TILES, False), []))
        plan = [1] * len(arrays)
        theirs = pl.pallas_call(
            partial(time_kernel, plan, 1, 0),
            grid=(1,),
            in_specs=[whole(SMEM), pl.BlockSpec((n_time, 2 * NF), lambda c: (1, 0))] + list(specs),
            out_specs=[still((n_time, OCT, TILE))],
            out_shape=[sds((n_time, OCT, TILE), bf16)],
            scratch_shapes=[VMEM((1, TILE // LANES, n_time * OCT, LANES), f32)],
            compiler_params=WIDE_PARAMS,
            cost_estimate=cost(0, 0),
            name="time_theirs",
        )(level, table, *arrays)[0]
        own = time_call(arrays, plan, list(specs), n_time, out, raw, 1, "time_own")[0]
        return own, theirs

    def late_time(q, out):
        sources = [lates[q], swaps_in[q], mids_in[q]]
        specs = [still(a.shape) for a in sources]
        wide = late_widths[q]
        return time_call(
            sources, [1] * 3, specs, 2 * n_time, out, late_first[q], 1, "time_late", wide
        )

    def raw_time(out):
        own, swap, mid, cross = chunk_sources(0, True)
        sources = own + swap
        for way, relayed in ((mid, near_out), (cross, far_out)):
            for k in range(CHUNKS):
                sources = sources + [way[k], (relayed[k], part(k, 0, 0, True))]
        arrays, specs = zip(*sources)
        plan = [1] * (2 * CHUNKS) + [2] * (2 * CHUNKS)
        return time_call(arrays, plan, list(specs), n_time, out, 0, RAW_TILES, "time_raw")[0]

    def place(j, got, out):
        return pl.pallas_call(
            partial(place_kernel, late_first[j - 1] if j else raw),
            in_specs=[whole(SMEM), whole(pl.ANY), whole(pl.ANY)],
            out_specs=whole(pl.ANY),
            out_shape=sds((n_time, OCT, width), bf16),
            input_output_aliases={2: 0},
            scratch_shapes=[VMEM(got.shape, bf16), pltpu.SemaphoreType.DMA(())],
            compiler_params=PARAMS,
            cost_estimate=cost(0, 3 * n_time * OCT * TILE * 2),
            name="place",
        )(outer, got, out)

    ends = [None] * (late + 1)
    swaps_in, mids_in = ([None] * late for _ in range(2))
    swaps_in[0] = send(lates[0], INWARD)
    crosses[last], far_out[last - 1], lates[1] = tie(crosses[last], far_out[last - 1], lates[1])
    far_out[last] = send(cut(crosses[last]), OUTWARD)
    out, theirs = early_time(None)
    swaps_in[0], theirs, lates[1] = tie(swaps_in[0], theirs, lates[1])
    theirs, near_out[last], far_out[last] = tie(theirs, near_out[last], far_out[last])
    ends[0] = send(theirs, OUTWARD)
    mids_in[0] = send(pack(lates[0], swaps_in[0], late_widths[0]), MIDDLE)
    swaps_in[1] = send(lates[1], INWARD)
    for q in range(late):
        if q:
            ends[q - 1], out = tie(ends[q - 1], out)
            out = place(q - 1, ends[q - 1], out)
        if q + 1 < late:
            swaps_in[q + 1], out = tie(swaps_in[q + 1], out)
            mids_in[q + 1] = send(pack(lates[q + 1], swaps_in[q + 1], late_widths[q + 1]), MIDDLE)
        if q + 2 < late:
            lates[q + 2], swaps_in[q + 1] = tie(lates[q + 2], swaps_in[q + 1])
            swaps_in[q + 2] = send(lates[q + 2], INWARD)
            mids_in[q], swaps_in[q + 2] = tie(mids_in[q], swaps_in[q + 2])
        if q == 1:
            out = raw_time(out)
        out, theirs = late_time(q, out)
        ends[q + 1] = send(theirs, OUTWARD)
    for j in range(late - 1, late + 1):
        out = place(j, ends[j], out)
    return out


def solution(mesh):
    line = mesh.shape["freq"] == 4 and mesh.shape["shot"] == 2 and mesh.shape["rcv"] == 2
    return jax.shard_map(
        line_body if line else general_body,
        mesh=mesh,
        in_specs=(
            P(None, "freq", ("grp", "shot"), "rcv"),
            P(None, "freq", ("grp", "shot"), "rcv"),
            P(None, "freq", ("grp", "shot"), None),
            P(None, ("grp", "freq")),
            P(("grp", "shot")),
            P("grp"),
            P("grp"),
            P("grp"),
        ),
        out_specs=P("freq", ("grp", "shot"), "rcv"),
        check_vma=False,
    )
```
